512 devices in a mesh: row: 32 (over z, x_lo), col: 16 (over x_hi, y, core).
Axes of the slice: x: 4 (x_hi: 2, x_lo: 2; x = x_hi * 2 + x_lo), y: 4, z: 16, core: 2. Of those that a mesh axis runs over, the one named last changes fastest.
Arguments:
- queries: bfloat16 [96, 1024, 128], P('row', 'col'), may hold values from -8 to 8
- keys: bfloat16 [96, 1024, 128], P('row', 'col'), may hold values from -8 to 8
- values: bfloat16 [96, 1024, 128], P('row', 'col'), may hold values from -6 to 6
- pair_mask: int32 [96, 1024], P('row', 'col'), may hold values 0 or 1
- tri_bias: bfloat16 [4, 1024, 1024], P(None, ('col', 'row')), may hold values from -8 to 400
- grad_out: bfloat16 [96, 1024, 128], P('row', 'col'), may hold values from -20 to 20
Outputs:
- query_grad: bfloat16 [96, 1024, 128], P('row', 'col')
- key_grad: bfloat16 [96, 1024, 128], P('row', 'col')
- value_grad: bfloat16 [96, 1024, 128], P('row', 'col')
- bias_grad: float32 [4, 1024, 1024], P(None, ('col', 'row'))
The draws below stay inside these ranges and needn't reach their ends.
All inputs are finite; a program needn't handle non-finite values. No bound on the sum of `pair_mask` on one device may be relied on, other than what follows from the above.
Results may differ from the reference program's by a relative error of at most 0.0051.
Values may be sent and summed in bfloat16 or wider, within the bound.
A program may use at most 64 MiB of HBM per device.

```python
import jax
import jax.numpy as jnp
from jax import lax

WIDTH = 128
HEADS = 4
HSIZE = 32
NR = 96
NC = 1024


def draw_tri_bias(key, part):
    key = jax.random.fold_in(key, 5)
    shape = (HEADS, NC, NC)
    return jnp.clip(1.5 * jax.random.normal(key, shape, jnp.float32), -8.0, 8.0).astype(jnp.bfloat16)


def with_ends(drawn, rng, smallest, high):
    longest = drawn.shape.index(max(drawn.shape))
    spots = []
    for shift in (0, 1):
        where = [jax.random.randint(jax.random.fold_in(rng, axis), (), 0, length) for axis, length in enumerate(drawn.shape)]
        where[longest] = (where[longest] + shift) % drawn.shape[longest]
        spots.append(tuple(where))
    return drawn.at[spots[0]].set(smallest).at[spots[1]].set(high)


def block_scale(key, extent, pieces, least, high):
    def one(axis_at, blocks):
        draws = jax.random.uniform(jax.random.fold_in(jax.random.fold_in(key, 6), axis_at), (blocks,), jnp.float32, least / len(pieces), high / len(pieces))
        return jnp.repeat(jnp.exp(draws), extent[axis_at] // blocks).reshape((-1,) + (1,) * (len(extent) - axis_at - 1))

    loudness = one(*pieces[0])
    for cut in pieces[1:]:
        loudness = loudness * one(*cut)
    return loudness


def normal_values(rng, shape, scale, limit, shards=(), kind=jnp.bfloat16):
    drawn = scale * jax.random.normal(rng, shape, jnp.float32)
    if shards:
        drawn = drawn * block_scale(rng, shape, shards, -0.22, 0.18)
    return jnp.clip(drawn, -limit, limit).astype(kind)


def setup_inputs(seed: int = 0) -> dict:
    seeds = jax.random.split(jax.random.key(seed), 7)
    queries = normal_values(seeds[0], (NR, NC, WIDTH), 1.4, 8.0, ((0, 32), (1, 16)))
    keys = normal_values(seeds[1], (NR, NC, WIDTH), 1.4, 8.0, ((0, 32), (1, 16)))
    values = normal_values(seeds[2], (NR, NC, WIDTH), 1.0, 6.0, ((0, 32), (1, 16)))
    pair_mask = with_ends((jax.random.randint(seeds[3], (NR, NC), 0, 16) < 15).astype(jnp.int32), jax.random.fold_in(seeds[3], 1), 0, 1)
    tri_bias = draw_tri_bias(jax.random.fold_in(seeds[6], 71), 0)
    grad_out = normal_values(seeds[5], (NR, NC, WIDTH), 4.0, 20.0, ((0, 32), (1, 16)))
    return dict(queries=queries, keys=keys, values=values, pair_mask=pair_mask, tri_bias=tri_bias, grad_out=grad_out)


def reference(queries, keys, values, pair_mask, tri_bias, grad_out):
    score_scale = HSIZE ** -0.5
    bias_wide = tri_bias.astype(jnp.float32)

    def one_row(bias_total, row_data):
        query_row, key_row, value_row, mask_row, grad_row = row_data
        query_heads = query_row.astype(jnp.float32).reshape(NC, HEADS, HSIZE)
        key_heads = key_row.astype(jnp.float32).reshape(NC, HEADS, HSIZE)
        value_heads = value_row.astype(jnp.float32).reshape(NC, HEADS, HSIZE)
        grad_heads = grad_row.astype(jnp.float32).reshape(NC, HEADS, HSIZE)
        penalty = 1e9 * (mask_row.astype(jnp.float32) - 1.0)
        scores = jnp.einsum('jhe,khe->hjk', query_heads, key_heads) * score_scale + bias_wide + penalty[None, None, :]
        maximum = jnp.max(scores, axis=-1, keepdims=True)
        expo = jnp.exp(scores - maximum)
        total_mass = jnp.sum(expo, axis=-1, keepdims=True)
        probs = expo / total_mass
        prob_grads = jnp.einsum('jhe,khe->hjk', grad_heads, value_heads)
        delta = jnp.sum(probs * prob_grads, axis=-1, keepdims=True)
        score_grads = probs * (prob_grads - delta)
        probs_low = lax.optimization_barrier(probs.astype(jnp.bfloat16)).astype(jnp.float32)
        score_low = lax.optimization_barrier(score_grads.astype(jnp.bfloat16)).astype(jnp.float32)
        query_grads = score_scale * jnp.einsum('hjk,khe->jhe', score_low, key_heads)
        key_grads = score_scale * jnp.einsum('hjk,jhe->khe', score_low, query_heads)
        value_grads = jnp.einsum('hjk,jhe->khe', probs_low, grad_heads)
        outputs = (query_grads.reshape(NC, WIDTH).astype(jnp.bfloat16),
                   key_grads.reshape(NC, WIDTH).astype(jnp.bfloat16),
                   value_grads.reshape(NC, WIDTH).astype(jnp.bfloat16))
        return bias_total + score_grads, outputs

    start = jnp.zeros((HEADS, NC, NC), jnp.float32)
    bias_grad, stacked = lax.scan(one_row, start, (queries, keys, values, pair_mask, grad_out))
    return stacked[0], stacked[1], stacked[2], bias_grad
```

```python
import functools

import jax
import jax.numpy as jnp
from jax import lax
from jax.experimental import pallas as pl
from jax.experimental.pallas import tpu as pltpu
from jax.sharding import PartitionSpec as P

MESH = pl.DeviceIdType.MESH
F32, BF16 = jnp.float32, jnp.bfloat16
SCALE = 32 ** -0.5
ROWS = 3
NT = (((1,), (1,)), ((), ()))
TN = (((0,), (0,)), ((), ()))


def iota(shape, dim):
    return lax.broadcasted_iota(jnp.int32, shape, dim)


def dot(a, b):
    return jnp.dot(a, b, preferred_element_type=F32)


def zero_one(hit):
    return jnp.where(hit, 1.0, 0.0).astype(BF16)


def class_place(at):
    return ((at >> 1) & 3) * 16 + (at >> 4) * 4 + ((at >> 3) & 1) * 2 + (at & 1)


def swap_place(at):
    return ((at >> 5) & 3) * 128 + (at >> 7) * 32 + (at & 31)


def half_place(at):
    return ((at >> 5) & 1) * 128 + (at >> 6) * 32 + (at & 31)


def kernel(
    q_ref, k_ref, v_ref, mask_ref, bias_ref, do_ref,
    dq_ref, dk_ref, dv_ref, dbias_ref,
    swap, kv_send, kv_recv, kv_roll, pen, qd_send, qd_recv, lhs, b_wide, b_send, b_all, b_f32,
    d_f32, d_send, d_recv, d_sum, e_recv, dkv_t, dkv_send, dkv_recv, dq_buf, dq_send, dq_recv,
    kv_ss, kv_rs, qd_ss, qd_rs, b1_ss, b1_rs, b2_ss, b2_rs,
    d2_ss, d2_rs, e_ss, e_rs, dkv_ss, dkv_rs, dq_ss, dq_rs,
):
    r, c = lax.axis_index("row"), lax.axis_index("col")
    z, xl = r // 2, r % 2
    y = (c // 2) % 4
    zq, kappa = z // 4, z % 4

    def at_z(dz, dxl):
        return ((z + dz + 16) % 16) * 2 + (xl + dxl) % 2

    def at_y(dy):
        return c + (((y + dy) % 4) - y) * 2

    def yz(o):
        dy, dz = o // 4, (o % 4) * 4
        return (y + dy) % 4, ((z + dz) % 16) // 4, (at_z(dz, 0), at_y(dy))

    def copy(src, dst, ss, rs, device):
        return pltpu.make_async_remote_copy(
            src_ref=src, dst_ref=dst, send_sem=ss, recv_sem=rs, device_id=device, device_id_type=MESH
        )

    def each(low, high, do):
        def body(o, carry):
            do(o)
            return carry

        lax.fori_loop(low, high, body, 0)

    near = [(0, 1)] + [(dz, dxl) for dz in (1, -1, 2, -2) for dxl in (0, 1)]
    barrier = pltpu.get_barrier_semaphore()

    def greet(device):
        pl.semaphore_signal(barrier, inc=1, device_id=device, device_id_type=MESH)

    def greet_yz(o):
        dy, dz = o % 4, (o // 4) * 4
        greet((at_z(dz, 0), at_y(dy)))

    each(4, 16, greet_yz)
    each(1, 16, lambda o: greet((r, (c + o) % 16)))
    for dz, dxl in near:
        greet((at_z(dz, dxl), c))

    wide = jnp.concatenate([bias_ref[h] for h in range(4)], axis=0)
    half_mat = zero_one(half_place(iota((256, 256), 0)) == iota((256, 256), 1))
    for m in range(4):
        turned = dot(wide[:, 256 * m:256 * (m + 1)], half_mat)
        for half in range(2):
            b_wide[pl.ds(half * 4 + m, 8, stride=8), :] = turned[:, 128 * half:128 * (half + 1)]
    b_send[...] = b_wide[...].astype(BF16).reshape(4, 16, 128)

    swap_mat = zero_one(swap_place(iota((512, 512), 0)) == iota((512, 512), 1))
    swap[...] = swap_mat
    spread = swap_mat[:256] + swap_mat[256:]
    low_lanes = iota((32, 128), 1) < 64
    mask_lane = (iota((8, 128), 1) >> 5) == c % 4
    mask = mask_ref[...].astype(F32)
    tiles = []
    for half in range(2):
        part = mask[:, 32 * half:32 * (half + 1)]
        part = jnp.concatenate([part] * 4, axis=1)
        part = jnp.concatenate([part, jnp.zeros((8 - ROWS, 128), F32)], axis=0)
        tiles.append(jnp.where(mask_lane, part, 0.0))
    mask_tile = jnp.concatenate(tiles, axis=0).astype(BF16)
    for h in range(4):
        kv_send[h, 96:112, :] = mask_tile
    for i in range(ROWS):
        pairs = dot(jnp.concatenate([k_ref[i], v_ref[i]], axis=1), spread)
        for h in range(4):
            one = pairs[:, 128 * h:128 * (h + 1)]
            kv_send[h, 32 * i:32 * (i + 1), :] = jnp.where(low_lanes, one[:32], one[32:]).astype(BF16)
    order = zero_one(class_place(iota((64, 64), 0)) == iota((64, 64), 1))
    low8 = iota((8, 128), 1) < 64
    for i in range(ROWS):
        turned = dot(order, jnp.concatenate([q_ref[i], do_ref[i]], axis=1)).astype(BF16)
        pairs = dot(turned, spread)
        for h in range(4):
            one = pairs[:, 128 * h:128 * (h + 1)]
            parts = [jnp.where(low8, one[16 * a:16 * a + 8], one[16 * a + 8:16 * a + 16]) for a in range(4)]
            qd_send[h, 32 * i:32 * (i + 1), :] = jnp.concatenate(parts, axis=0).astype(BF16)

    pl.semaphore_wait(barrier, 12 + 15 + len(near))

    def b1(o):
        to_y, _, device = yz(o)
        return copy(b_send.at[to_y], b_all.at[kappa, xl, y * 4 + zq], b1_ss.at[o], b1_rs.at[o], device)

    def kv(o):
        to = (c + o) % 16
        return copy(kv_send.at[(to // 2) % 4], kv_recv.at[c], kv_ss.at[o], kv_rs.at[o], (r, to))

    def qd(o):
        return copy(qd_send.at[(y + o) % 4], qd_recv.at[y], qd_ss.at[o], qd_rs.at[o], (r, at_y(o)))

    each(1, 16, lambda o: b1(o).start())
    each(1, 4, lambda o: qd(o).start())
    each(1, 16, lambda o: kv(o).start())
    b_all[kappa, xl, y * 4 + zq] = b_send[y]
    kv_recv[c] = kv_send[y]
    qd_recv[y] = qd_send[y]

    each(1, 16, lambda o: b1(o).wait_recv())

    def b2(j):
        dz, dxl = near[j]
        mine = b_all.at[kappa, xl]
        if dz == 2:
            mine = mine.at[pl.ds(0, 8)]
        elif dz == -2:
            mine = mine.at[pl.ds(8, 8)]
        return copy(mine, mine, b2_ss.at[j], b2_rs.at[j], (at_z(dz, dxl), c))

    for j in range(len(near)):
        b2(j).start()

    each(1, 4, lambda o: qd(o).wait_recv())
    lane_part = iota((64, 128), 1) >> 5
    for i in range(ROWS):
        plain = [qd_recv[p, 32 * i:32 * (i + 1), :].astype(F32) for p in range(4)]
        rolled = [jnp.concatenate([one[:, 64:], one[:, :64]], axis=1) for one in plain]
        for a in range(4):
            first = jnp.concatenate([one[8 * a:8 * a + 8] for one in plain], axis=0)
            other = jnp.concatenate([one[8 * a:8 * a + 8] for one in rolled], axis=0)
            straight = jnp.concatenate([first, other], axis=0)
            crossed = jnp.concatenate([other, first], axis=0)
            for part in range(4):
                block = straight if part < 2 else crossed
                lhs[a, i, 64 * part:64 * (part + 1), :] = jnp.where(lane_part == part, block, 0.0).astype(BF16)

    each(1, 16, lambda o: kv(o).wait_recv())
    for g in range(4):
        seen = jnp.zeros((16, 128), F32)
        for u in range(4):
            seen = seen + kv_recv[4 * g + u, 96:112, :].astype(F32)
        pen[:, 128 * g:128 * (g + 1)] = 1e9 * (seen - 1.0)
    for i in range(ROWS):
        block = kv_recv[:, 32 * i:32 * (i + 1), :]
        kv_roll[i] = jnp.concatenate([block[:, :, 64:], block[:, :, :64]], axis=2).reshape(512, 128)

    def class_step(step, delta, waits):
        cls = (kappa + delta) % 4
        for j in waits:
            b2(j).wait_recv()
        b_f32[...] = b_all[cls].astype(F32).reshape(512, 128)
        keep = d_f32.at[0 if step == 0 else 1]

        def row(i, carry):
            left = lhs[cls, i]
            right = kv_recv[:, pl.ds(pl.multiple_of(i * 32, 32), 32), :].reshape(512, 128)
            both = lax.dot_general(left, right, NT, preferred_element_type=F32)
            bias_a = jnp.concatenate([b_f32[pl.ds(m, 64, stride=8), :] for m in range(4)], axis=1)
            bias_b = jnp.concatenate([b_f32[pl.ds(m, 64, stride=8), :] for m in range(4, 8)], axis=1)
            s_a = both[0:64] * SCALE + bias_a + pen[pl.ds(i, 1), :]
            s_b = both[128:192] * SCALE + bias_b + pen[pl.ds(i + 8, 1), :]
            dp_a, dp_b = both[64:128], both[192:256]
            top = jnp.max(jnp.maximum(s_a, s_b), axis=1, keepdims=True)
            e_a, e_b = jnp.exp(s_a - top), jnp.exp(s_b - top)
            inv = 1.0 / jnp.sum(e_a + e_b, axis=1, keepdims=True)
            delta_row = jnp.sum(e_a * dp_a + e_b * dp_b, axis=1, keepdims=True) * inv
            p_a, p_b = e_a * inv, e_b * inv
            g_a, g_b = p_a * (dp_a - delta_row), p_b * (dp_b - delta_row)
            for m in range(8):
                one = (g_a if m < 4 else g_b)[:, 128 * (m % 4):128 * (m % 4 + 1)]
                at = pl.ds(m, 64, stride=8)
                keep[at, :] = jnp.where(i == 0, 0.0, keep[at, :]) + one
            g_a, g_b = g_a.astype(BF16), g_b.astype(BF16)
            stack = jnp.concatenate([g_a, p_a.astype(BF16), g_b, p_b.astype(BF16)], axis=0)
            turned = lax.dot_general(left, stack, TN, preferred_element_type=F32)
            if step == 0:
                dkv_t[i] = turned
            else:
                dkv_t[i] += turned
            dq_buf[cls, i] = dot(g_a, right) + dot(g_b, kv_roll[i])
            return carry

        lax.fori_loop(0, ROWS, row, 0)
        d_send[step] = keep[...].astype(BF16).reshape(2, 16, 16, 128)

    def d2(j):
        dz, dxl = near[j]
        step = {0: 0, 1: 1, -1: 2, 2: 3, -2: 3}[dz]
        src, dst = d_send.at[step, (xl + dxl) % 2], d_recv.at[dxl, step]
        if dz in (2, -2):
            half = pl.ds(0, 8) if dz == 2 else pl.ds(8, 8)
            src, dst = src.at[half], dst.at[half]
        return copy(src, dst, d2_ss.at[j], d2_rs.at[j], (at_z(dz, dxl), c))

    index = {pair: j for j, pair in enumerate(near)}
    plan = [(0, [(0, 1)]), (1, [(-1, 0), (-1, 1)]), (3, [(1, 0), (1, 1)]), (2, [(2, 0), (2, 1), (-2, 0), (-2, 1)])]
    outs = [[(0, 1)], [(1, 0), (1, 1)], [(-1, 0), (-1, 1)], [(2, 0), (2, 1), (-2, 0), (-2, 1)]]
    for step, (delta, waits) in enumerate(plan):
        class_step(step, delta, [index[w] for w in waits])
        for w in outs[step]:
            d2(index[w]).start()

    for i in range(ROWS):
        for b in range(4):
            turned = dkv_t[i, :, 128 * b:128 * (b + 1)].T
            dkv_send[4 * b:4 * b + 4, 32 * i:32 * (i + 1), :] = turned.reshape(4, 32, 128).astype(dkv_send.dtype)

    def dkv(o):
        to = (c + o) % 16
        return copy(dkv_send.at[to], dkv_recv.at[c], dkv_ss.at[o], dkv_rs.at[o], (r, to))

    each(1, 16, lambda o: dkv(o).start())
    dkv_recv[c] = dkv_send[c]

    gather = zero_one(
        ((iota((512, 128), 0) >> 7) * 32 + (iota((512, 128), 0) & 127)) == iota((512, 128), 1)
    )
    gather = jnp.where((iota((512, 128), 0) & 127) < 32, gather, jnp.zeros_like(gather))
    packed = []
    for i in range(ROWS):
        row = jnp.concatenate([(dq_buf[a, i] * SCALE).astype(BF16) for a in range(4)], axis=1)
        packed.append(dot(row, gather))
    for p in range(4):
        pieces = [packed[i][32 * x + 8 * p:32 * x + 8 * p + 8] for i in range(ROWS) for x in range(2)]
        dq_send[p] = jnp.concatenate(pieces, axis=0).astype(BF16)

    def dq(o):
        return copy(dq_send.at[(y + o) % 4], dq_recv.at[y], dq_ss.at[o], dq_rs.at[o], (r, at_y(o)))

    each(1, 4, lambda o: dq(o).start())
    dq_recv[y] = dq_send[y]

    for j in range(len(near)):
        d2(j).wait_recv()
    total = d_f32[0, pl.ds(pl.multiple_of(xl * 256, 256), 256), :]
    for dxl in range(2):
        for slot in range(4):
            if dxl or slot:
                total = total + d_recv[dxl, slot].astype(F32).reshape(256, 128)
    d_sum[...] = total.reshape(16, 16, 128)

    def e(o):
        to_y, to_zq, device = yz(o)
        return copy(d_sum.at[to_y * 4 + to_zq], e_recv.at[y, zq], e_ss.at[o], e_rs.at[o], device)

    each(1, 16, lambda o: e(o).start())
    e_recv[y, zq] = d_sum[y * 4 + zq]

    each(1, 4, lambda o: dq(o).wait_recv())
    back = zero_one(iota((64, 64), 0) == class_place(iota((64, 64), 1)))
    heads = dot(jnp.concatenate([dq_recv[h] for h in range(4)], axis=1), swap[...]).astype(BF16)
    for i in range(ROWS):
        block = jnp.concatenate([heads[16 * i:16 * (i + 1), 128 * a:128 * (a + 1)] for a in range(4)], axis=0)
        dq_ref[i] = dot(back, block).astype(BF16)

    each(1, 16, lambda o: dkv(o).wait_recv())
    k_lanes = ((iota((96, 128), 1) >> 5) & 1) == 0
    sums = []
    for h in range(4):
        one = jnp.zeros((96, 128), F32)
        for x in range(2):
            for core in range(2):
                one = one + dkv_recv[x * 8 + h * 2 + core].astype(F32)
        sums.append(jnp.where(k_lanes, one * SCALE, one).astype(BF16))
    heads = dot(jnp.concatenate(sums, axis=1), swap[...]).astype(BF16)
    for i in range(ROWS):
        for half in range(2):
            part = heads[32 * i:32 * (i + 1), 256 * half:256 * (half + 1)]
            dk_ref[i, 32 * half:32 * (half + 1), :] = part[:, :128]
            dv_ref[i, 32 * half:32 * (half + 1), :] = part[:, 128:]

    each(1, 16, lambda o: e(o).wait_recv())
    total = e_recv[:, 0] + e_recv[:, 1] + e_recv[:, 2] + e_recv[:, 3]
    b_wide[...] = total.reshape(64, 128)
    half_back = jnp.where(iota((256, 256), 0) == half_place(iota((256, 256), 1)), 1.0, 0.0)
    for m in range(4):
        pair = jnp.concatenate([b_wide[pl.ds(half * 4 + m, 8, stride=8), :] for half in range(2)], axis=1)
        turned = jnp.dot(pair, half_back, precision=lax.Precision.HIGHEST, preferred_element_type=F32)
        for h in range(4):
            dbias_ref[h, :, 256 * m:256 * (m + 1)] = turned[2 * h:2 * h + 2]

    each(1, 16, lambda o: b1(o).wait_send())
    each(1, 16, lambda o: kv(o).wait_send())
    each(1, 4, lambda o: qd(o).wait_send())
    for j in range(len(near)):
        b2(j).wait_send()
        d2(j).wait_send()
    each(1, 16, lambda o: dkv(o).wait_send())
    each(1, 4, lambda o: dq(o).wait_send())
    each(1, 16, lambda o: e(o).wait_send())


def on_device(queries, keys, values, pair_mask, tri_bias, grad_out):
    sem = pltpu.SemaphoreType.DMA
    vmem = pl.BlockSpec(memory_space=pltpu.VMEM)
    tile = (16, 128)
    return pl.pallas_call(
        kernel,
        name="attention_backward",
        out_shape=(
            jax.ShapeDtypeStruct(queries.shape, BF16),
            jax.ShapeDtypeStruct(keys.shape, BF16),
            jax.ShapeDtypeStruct(values.shape, BF16),
            jax.ShapeDtypeStruct(tri_bias.shape, F32),
        ),
        in_specs=[vmem] * 6,
        out_specs=[vmem] * 4,
        scratch_shapes=[
            pltpu.VMEM((512, 512), BF16),
            pltpu.VMEM((4, 112, 128), BF16),
            pltpu.VMEM((16, 112, 128), BF16),
            pltpu.VMEM((ROWS, 512, 128), BF16),
            pltpu.VMEM((16, 512), F32),
            pltpu.VMEM((4, 96, 128), BF16),
            pltpu.VMEM((4, 96, 128), BF16),
            pltpu.VMEM((4, ROWS, 256, 128), BF16),
            pltpu.VMEM((64, 128), F32),
            pltpu.VMEM((4,) + tile, BF16),
            pltpu.VMEM((4, 2, 16) + tile, BF16),
            pltpu.VMEM((512, 128), F32),
            pltpu.VMEM((2, 512, 128), F32),
            pltpu.VMEM((4, 2, 16) + tile, BF16),
            pltpu.VMEM((2, 4, 16) + tile, BF16),
            pltpu.VMEM((16,) + tile, F32),
            pltpu.VMEM((4, 4) + tile, F32),
            pltpu.VMEM((ROWS, 128, 512), F32),
            pltpu.VMEM((16, 96, 128), BF16),
            pltpu.VMEM((16, 96, 128), BF16),
            pltpu.VMEM((4, ROWS, 64, 128), F32),
            pltpu.VMEM((4, 48, 128), BF16),
            pltpu.VMEM((4, 48, 128), BF16),
            sem((16,)), sem((16,)), sem((4,)), sem((4,)), sem((16,)), sem((16,)), sem((9,)), sem((9,)),
            sem((9,)), sem((9,)), sem((16,)), sem((16,)), sem((16,)), sem((16,)), sem((4,)), sem((4,)),
        ],
        compiler_params=pltpu.CompilerParams(
            collective_id=0, has_side_effects=True, vmem_limit_bytes=40 * 1024 * 1024
        ),
    )(queries, keys, values, pair_mask, tri_bias, grad_out)


def solution(mesh):
    pair = P("row", "col", None)
    bias = P(None, ("col", "row"), None)
    return jax.shard_map(
        on_device,
        mesh=mesh,
        in_specs=(pair, pair, pair, P("row", "col"), bias, pair),
        out_specs=(pair, pair, pair, bias),
        check_vma=False,
    )
```

```python
import functools

import jax
import jax.numpy as jnp
from jax import lax
from jax.experimental import pallas as pl
from jax.experimental.pallas import tpu as pltpu
from jax.sharding import PartitionSpec as P

MESH = pl.DeviceIdType.MESH
F32, BF16 = jnp.float32, jnp.bfloat16
SCALE = 32 ** -0.5
ROWS = 3
NT = (((1,), (1,)), ((), ()))
TN = (((0,), (0,)), ((), ()))


def iota(shape, dim):
    return lax.broadcasted_iota(jnp.int32, shape, dim)


def dot(a, b):
    return jnp.dot(a, b, preferred_element_type=F32)


def zero_one(hit):
    return jnp.where(hit, 1.0, 0.0).astype(BF16)


def class_place(at):
    return ((at >> 1) & 3) * 16 + (at >> 4) * 4 + ((at >> 3) & 1) * 2 + (at & 1)


def swap_place(at):
    return ((at >> 5) & 3) * 128 + (at >> 7) * 32 + (at & 31)


def half_place(at):
    return ((at >> 5) & 1) * 128 + (at >> 6) * 32 + (at & 31)


def kernel(
    q_hbm, k_hbm, v_hbm, mask_hbm, bias_hbm, do_hbm,
    dq_hbm, dk_hbm, dv_hbm, dbias_hbm,
    dq_ref, dk_ref, dv_ref, dbias_ref, q_ref, k_ref, v_ref, mask_ref, bias_ref, do_ref,
    swap, kv_send, kv_recv, kv_roll, pen, qd_send, qd_recv, lhs, b_wide, b_send, b_all, b_f32,
    d_f32, d_send, d_recv, d_sum, e_recv, dkv_t, dkv_send, dkv_recv, dq_buf, dq_send, dq_recv,
    in_sem, out_sem, kv_ss, kv_rs, qd_ss, qd_rs, b1_ss, b1_rs, b2_ss, b2_rs,
    d2_ss, d2_rs, e_ss, e_rs, dkv_ss, dkv_rs, dq_ss, dq_rs,
):
    r, c = lax.axis_index("row"), lax.axis_index("col")
    z, xl = r // 2, r % 2
    y = (c // 2) % 4
    zq, kappa = z // 4, z % 4

    def at_z(dz, dxl):
        return ((z + dz + 16) % 16) * 2 + (xl + dxl) % 2

    def at_y(dy):
        return c + (((y + dy) % 4) - y) * 2

    def yz(o):
        dy, dz = o // 4, (o % 4) * 4
        return (y + dy) % 4, ((z + dz) % 16) // 4, (at_z(dz, 0), at_y(dy))

    def copy(src, dst, ss, rs, device):
        return pltpu.make_async_remote_copy(
            src_ref=src, dst_ref=dst, send_sem=ss, recv_sem=rs, device_id=device, device_id_type=MESH
        )

    def each(low, high, do):
        def body(o, carry):
            do(o)
            return carry

        lax.fori_loop(low, high, body, 0)

    loads = [
        pltpu.make_async_copy(src, dst, in_sem.at[j])
        for j, (src, dst) in enumerate((
            (bias_hbm, bias_ref), (k_hbm, k_ref), (v_hbm, v_ref), (mask_hbm, mask_ref), (q_hbm, q_ref), (do_hbm, do_ref),
        ))
    ]
    for load in loads:
        load.start()

    near = [(0, 1)] + [(dz, dxl) for dz in (1, -1, 2, -2) for dxl in (0, 1)]
    barrier = pltpu.get_barrier_semaphore()

    def greet(device):
        pl.semaphore_signal(barrier, inc=1, device_id=device, device_id_type=MESH)

    def greet_yz(o):
        dy, dz = o % 4, (o // 4) * 4
        greet((at_z(dz, 0), at_y(dy)))

    each(4, 16, greet_yz)
    each(1, 16, lambda o: greet((r, (c + o) % 16)))
    for dz, dxl in near:
        greet((at_z(dz, dxl), c))

    loads[0].wait()
    wide = jnp.concatenate([bias_ref[h] for h in range(4)], axis=0)
    half_mat = zero_one(half_place(iota((256, 256), 0)) == iota((256, 256), 1))
    for m in range(4):
        turned = dot(wide[:, 256 * m:256 * (m + 1)], half_mat)
        for half in range(2):
            b_wide[pl.ds(half * 4 + m, 8, stride=8), :] = turned[:, 128 * half:128 * (half + 1)]
    b_send[...] = b_wide[...].astype(BF16).reshape(4, 16, 128)

    swap_mat = zero_one(swap_place(iota((512, 512), 0)) == iota((512, 512), 1))
    swap[...] = swap_mat
    spread = swap_mat[:256] + swap_mat[256:]
    for load in loads[1:]:
        load.wait()
    low_lanes = iota((32, 128), 1) < 64
    mask_lane = (iota((8, 128), 1) >> 5) == c % 4
    mask = mask_ref[...].astype(F32)
    tiles = []
    for half in range(2):
        part = mask[:, 32 * half:32 * (half + 1)]
        part = jnp.concatenate([part] * 4, axis=1)
        part = jnp.concatenate([part, jnp.zeros((8 - ROWS, 128), F32)], axis=0)
        tiles.append(jnp.where(mask_lane, part, 0.0))
    mask_tile = jnp.concatenate(tiles, axis=0).astype(BF16)
    for h in range(4):
        kv_send[h, 96:112, :] = mask_tile
    for i in range(ROWS):
        pairs = dot(jnp.concatenate([k_ref[i], v_ref[i]], axis=1), spread)
        for h in range(4):
            one = pairs[:, 128 * h:128 * (h + 1)]
            kv_send[h, 32 * i:32 * (i + 1), :] = jnp.where(low_lanes, one[:32], one[32:]).astype(BF16)
    order = zero_one(class_place(iota((64, 64), 0)) == iota((64, 64), 1))
    low8 = iota((8, 128), 1) < 64
    for i in range(ROWS):
        turned = dot(order, jnp.concatenate([q_ref[i], do_ref[i]], axis=1)).astype(BF16)
        pairs = dot(turned, spread)
        for h in range(4):
            one = pairs[:, 128 * h:128 * (h + 1)]
            parts = [jnp.where(low8, one[16 * a:16 * a + 8], one[16 * a + 8:16 * a + 16]) for a in range(4)]
            qd_send[h, 32 * i:32 * (i + 1), :] = jnp.concatenate(parts, axis=0).astype(BF16)

    pl.semaphore_wait(barrier, 12 + 15 + len(near))

    def b1(o):
        to_y, _, device = yz(o)
        return copy(b_send.at[to_y], b_all.at[kappa, xl, y * 4 + zq], b1_ss.at[o], b1_rs.at[o], device)

    def kv(o):
        to = (c + o) % 16
        return copy(kv_send.at[(to // 2) % 4], kv_recv.at[c], kv_ss.at[o], kv_rs.at[o], (r, to))

    def qd(o):
        return copy(qd_send.at[(y + o) % 4], qd_recv.at[y], qd_ss.at[o], qd_rs.at[o], (r, at_y(o)))

    each(1, 16, lambda o: b1(o).start())
    each(1, 4, lambda o: qd(o).start())
    each(1, 16, lambda o: kv(o).start())
    b_all[kappa, xl, y * 4 + zq] = b_send[y]
    kv_recv[c] = kv_send[y]
    qd_recv[y] = qd_send[y]

    each(1, 16, lambda o: b1(o).wait_recv())

    def b2(j):
        dz, dxl = near[j]
        mine = b_all.at[kappa, xl]
        if dz == 2:
            mine = mine.at[pl.ds(0, 8)]
        elif dz == -2:
            mine = mine.at[pl.ds(8, 8)]
        return copy(mine, mine, b2_ss.at[j], b2_rs.at[j], (at_z(dz, dxl), c))

    for j in range(len(near)):
        b2(j).start()

    each(1, 4, lambda o: qd(o).wait_recv())
    lane_part = iota((64, 128), 1) >> 5
    for i in range(ROWS):
        plain = [qd_recv[p, 32 * i:32 * (i + 1), :].astype(F32) for p in range(4)]
        rolled = [jnp.concatenate([one[:, 64:], one[:, :64]], axis=1) for one in plain]
        for a in range(4):
            first = jnp.concatenate([one[8 * a:8 * a + 8] for one in plain], axis=0)
            other = jnp.concatenate([one[8 * a:8 * a + 8] for one in rolled], axis=0)
            straight = jnp.concatenate([first, other], axis=0)
            crossed = jnp.concatenate([other, first], axis=0)
            for part in range(4):
                block = straight if part < 2 else crossed
                lhs[a, i, 64 * part:64 * (part + 1), :] = jnp.where(lane_part == part, block, 0.0).astype(BF16)

    each(1, 16, lambda o: kv(o).wait_recv())
    for g in range(4):
        seen = jnp.zeros((16, 128), F32)
        for u in range(4):
            seen = seen + kv_recv[4 * g + u, 96:112, :].astype(F32)
        pen[:, 128 * g:128 * (g + 1)] = 1e9 * (seen - 1.0)
    for i in range(ROWS):
        block = kv_recv[:, 32 * i:32 * (i + 1), :]
        kv_roll[i] = jnp.concatenate([block[:, :, 64:], block[:, :, :64]], axis=2).reshape(512, 128)

    def class_step(step, delta, waits):
        cls = (kappa + delta) % 4
        for j in waits:
            b2(j).wait_recv()
        b_f32[...] = b_all[cls].astype(F32).reshape(512, 128)
        keep = d_f32.at[0 if step == 0 else 1]

        def row(i, carry):
            left = lhs[cls, i]
            right = kv_recv[:, pl.ds(pl.multiple_of(i * 32, 32), 32), :].reshape(512, 128)
            both = lax.dot_general(left, right, NT, preferred_element_type=F32)
            bias_a = jnp.concatenate([b_f32[pl.ds(m, 64, stride=8), :] for m in range(4)], axis=1)
            bias_b = jnp.concatenate([b_f32[pl.ds(m, 64, stride=8), :] for m in range(4, 8)], axis=1)
            s_a = both[0:64] * SCALE + bias_a + pen[pl.ds(i, 1), :]
            s_b = both[128:192] * SCALE + bias_b + pen[pl.ds(i + 8, 1), :]
            dp_a, dp_b = both[64:128], both[192:256]
            top = jnp.max(jnp.maximum(s_a, s_b), axis=1, keepdims=True)
            e_a, e_b = jnp.exp(s_a - top), jnp.exp(s_b - top)
            inv = 1.0 / jnp.sum(e_a + e_b, axis=1, keepdims=True)
            delta_row = jnp.sum(e_a * dp_a + e_b * dp_b, axis=1, keepdims=True) * inv
            p_a, p_b = e_a * inv, e_b * inv
            g_a, g_b = p_a * (dp_a - delta_row), p_b * (dp_b - delta_row)
            for m in range(8):
                one = (g_a if m < 4 else g_b)[:, 128 * (m % 4):128 * (m % 4 + 1)]
                at = pl.ds(m, 64, stride=8)
                keep[at, :] = jnp.where(i == 0, 0.0, keep[at, :]) + one
            g_a, g_b = g_a.astype(BF16), g_b.astype(BF16)
            stack = jnp.concatenate([g_a, p_a.astype(BF16), g_b, p_b.astype(BF16)], axis=0)
            turned = lax.dot_general(left, stack, TN, preferred_element_type=F32)
            if step == 0:
                dkv_t[i] = turned
            else:
                dkv_t[i] += turned
            dq_buf[cls, i] = dot(g_a, right) + dot(g_b, kv_roll[i])
            return carry

        lax.fori_loop(0, ROWS, row, 0)
        d_send[step] = keep[...].astype(BF16).reshape(2, 16, 16, 128)

    def d2(j):
        dz, dxl = near[j]
        step = {0: 0, 1: 1, -1: 2, 2: 3, -2: 3}[dz]
        src, dst = d_send.at[step, (xl + dxl) % 2], d_recv.at[dxl, step]
        if dz in (2, -2):
            half = pl.ds(0, 8) if dz == 2 else pl.ds(8, 8)
            src, dst = src.at[half], dst.at[half]
        return copy(src, dst, d2_ss.at[j], d2_rs.at[j], (at_z(dz, dxl), c))

    index = {pair: j for j, pair in enumerate(near)}
    plan = [(0, [(0, 1)]), (1, [(-1, 0), (-1, 1)]), (3, [(1, 0), (1, 1)]), (2, [(2, 0), (2, 1), (-2, 0), (-2, 1)])]
    outs = [[(0, 1)], [(1, 0), (1, 1)], [(-1, 0), (-1, 1)], [(2, 0), (2, 1), (-2, 0), (-2, 1)]]
    for step, (delta, waits) in enumerate(plan):
        class_step(step, delta, [index[w] for w in waits])
        for w in outs[step]:
            d2(index[w]).start()

    for i in range(ROWS):
        for b in range(4):
            turned = dkv_t[i, :, 128 * b:128 * (b + 1)].T
            dkv_send[4 * b:4 * b + 4, 32 * i:32 * (i + 1), :] = turned.reshape(4, 32, 128).astype(dkv_send.dtype)

    def dkv(o):
        to = (c + o) % 16
        return copy(dkv_send.at[to], dkv_recv.at[c], dkv_ss.at[o], dkv_rs.at[o], (r, to))

    each(1, 16, lambda o: dkv(o).start())
    dkv_recv[c] = dkv_send[c]

    gather = zero_one(
        ((iota((512, 128), 0) >> 7) * 32 + (iota((512, 128), 0) & 127)) == iota((512, 128), 1)
    )
    gather = jnp.where((iota((512, 128), 0) & 127) < 32, gather, jnp.zeros_like(gather))
    packed = []
    for i in range(ROWS):
        row = jnp.concatenate([(dq_buf[a, i] * SCALE).astype(BF16) for a in range(4)], axis=1)
        packed.append(dot(row, gather))
    for p in range(4):
        pieces = [packed[i][32 * x + 8 * p:32 * x + 8 * p + 8] for i in range(ROWS) for x in range(2)]
        dq_send[p] = jnp.concatenate(pieces, axis=0).astype(BF16)

    def dq(o):
        return copy(dq_send.at[(y + o) % 4], dq_recv.at[y], dq_ss.at[o], dq_rs.at[o], (r, at_y(o)))

    each(1, 4, lambda o: dq(o).start())
    dq_recv[y] = dq_send[y]

    for j in range(len(near)):
        d2(j).wait_recv()
    total = d_f32[0, pl.ds(pl.multiple_of(xl * 256, 256), 256), :]
    for dxl in range(2):
        for slot in range(4):
            if dxl or slot:
                total = total + d_recv[dxl, slot].astype(F32).reshape(256, 128)
    d_sum[...] = total.reshape(16, 16, 128).astype(BF16)

    def e(o):
        to_y, to_zq, device = yz(o)
        return copy(d_sum.at[to_y * 4 + to_zq], e_recv.at[y, zq], e_ss.at[o], e_rs.at[o], device)

    each(1, 16, lambda o: e(o).start())
    e_recv[y, zq] = d_sum[y * 4 + zq]

    each(1, 4, lambda o: dq(o).wait_recv())
    back = zero_one(iota((64, 64), 0) == class_place(iota((64, 64), 1)))
    heads = dot(jnp.concatenate([dq_recv[h] for h in range(4)], axis=1), swap[...]).astype(BF16)
    for i in range(ROWS):
        block = jnp.concatenate([heads[16 * i:16 * (i + 1), 128 * a:128 * (a + 1)] for a in range(4)], axis=0)
        dq_ref[i] = dot(back, block).astype(BF16)
    stores = [
        pltpu.make_async_copy(src, dst, out_sem.at[j])
        for j, (src, dst) in enumerate(((dq_ref, dq_hbm), (dk_ref, dk_hbm), (dv_ref, dv_hbm), (dbias_ref, dbias_hbm)))
    ]
    stores[0].start()

    each(1, 16, lambda o: dkv(o).wait_recv())
    k_lanes = ((iota((96, 128), 1) >> 5) & 1) == 0
    sums = []
    for h in range(4):
        one = jnp.zeros((96, 128), F32)
        for x in range(2):
            for core in range(2):
                one = one + dkv_recv[x * 8 + h * 2 + core].astype(F32)
        sums.append(jnp.where(k_lanes, one * SCALE, one).astype(BF16))
    heads = dot(jnp.concatenate(sums, axis=1), swap[...]).astype(BF16)
    for i in range(ROWS):
        for half in range(2):
            part = heads[32 * i:32 * (i + 1), 256 * half:256 * (half + 1)]
            dk_ref[i, 32 * half:32 * (half + 1), :] = part[:, :128]
            dv_ref[i, 32 * half:32 * (half + 1), :] = part[:, 128:]

    stores[1].start()
    stores[2].start()

    each(1, 16, lambda o: e(o).wait_recv())
    total = sum(e_recv[:, part].astype(F32) for part in range(4))
    b_wide[...] = total.reshape(64, 128)
    half_back = jnp.where(iota((256, 256), 0) == half_place(iota((256, 256), 1)), 1.0, 0.0)
    for m in range(4):
        pair = jnp.concatenate([b_wide[pl.ds(half * 4 + m, 8, stride=8), :] for half in range(2)], axis=1)
        turned = jnp.dot(pair, half_back, precision=lax.Precision.HIGHEST, preferred_element_type=F32)
        for h in range(4):
            dbias_ref[h, :, 256 * m:256 * (m + 1)] = turned[2 * h:2 * h + 2]

    stores[3].start()

    each(1, 16, lambda o: b1(o).wait_send())
    each(1, 16, lambda o: kv(o).wait_send())
    each(1, 4, lambda o: qd(o).wait_send())
    for j in range(len(near)):
        b2(j).wait_send()
        d2(j).wait_send()
    each(1, 16, lambda o: dkv(o).wait_send())
    each(1, 4, lambda o: dq(o).wait_send())
    each(1, 16, lambda o: e(o).wait_send())
    for one in stores:
        one.wait()


def store(*refs):
    ins, outs, sems = refs[:4], refs[4:8], refs[8]
    copies = [pltpu.make_async_copy(src, dst, sems.at[j]) for j, (src, dst) in enumerate(zip(ins, outs))]
    for one in copies:
        one.start()
    for one in copies:
        one.wait()


def on_device(queries, keys, values, pair_mask, tri_bias, grad_out):
    sem = pltpu.SemaphoreType.DMA
    hbm = pl.BlockSpec(memory_space=pltpu.HBM)
    tile = (16, 128)
    shapes = (
        jax.ShapeDtypeStruct(queries.shape, BF16),
        jax.ShapeDtypeStruct(keys.shape, BF16),
        jax.ShapeDtypeStruct(values.shape, BF16),
        jax.ShapeDtypeStruct(tri_bias.shape, F32),
    )
    grads = pl.pallas_call(
        kernel,
        name="attention_backward",
        out_shape=shapes,
        in_specs=[hbm] * 6,
        out_specs=[hbm] * 4,
        scratch_shapes=[
            pltpu.VMEM(queries.shape, BF16),
            pltpu.VMEM(keys.shape, BF16),
            pltpu.VMEM(values.shape, BF16),
            pltpu.VMEM(tri_bias.shape, F32),
            pltpu.VMEM(queries.shape, BF16),
            pltpu.VMEM(keys.shape, BF16),
            pltpu.VMEM(values.shape, BF16),
            pltpu.VMEM(pair_mask.shape, jnp.int32),
            pltpu.VMEM(tri_bias.shape, BF16),
            pltpu.VMEM(grad_out.shape, BF16),
            pltpu.VMEM((512, 512), BF16),
            pltpu.VMEM((4, 112, 128), BF16),
            pltpu.VMEM((16, 112, 128), BF16),
            pltpu.VMEM((ROWS, 512, 128), BF16),
            pltpu.VMEM((16, 512), F32),
            pltpu.VMEM((4, 96, 128), BF16),
            pltpu.VMEM((4, 96, 128), BF16),
            pltpu.VMEM((4, ROWS, 256, 128), BF16),
            pltpu.VMEM((64, 128), F32),
            pltpu.VMEM((4,) + tile, BF16),
            pltpu.VMEM((4, 2, 16) + tile, BF16),
            pltpu.VMEM((512, 128), F32),
            pltpu.VMEM((2, 512, 128), F32),
            pltpu.VMEM((4, 2, 16) + tile, BF16),
            pltpu.VMEM((2, 4, 16) + tile, BF16),
            pltpu.VMEM((16,) + tile, BF16),
            pltpu.VMEM((4, 4) + tile, BF16),
            pltpu.VMEM((ROWS, 128, 512), F32),
            pltpu.VMEM((16, 96, 128), BF16),
            pltpu.VMEM((16, 96, 128), BF16),
            pltpu.VMEM((4, ROWS, 64, 128), F32),
            pltpu.VMEM((4, 48, 128), BF16),
            pltpu.VMEM((4, 48, 128), BF16),
            sem((6,)), sem((4,)), sem((16,)), sem((16,)), sem((4,)), sem((4,)), sem((16,)), sem((16,)), sem((9,)), sem((9,)),
            sem((9,)), sem((9,)), sem((16,)), sem((16,)), sem((16,)), sem((16,)), sem((4,)), sem((4,)),
        ],
        compiler_params=pltpu.CompilerParams(
            collective_id=0, has_side_effects=True, vmem_limit_bytes=60 * 1024 * 1024
        ),
    )(queries, keys, values, pair_mask, tri_bias, grad_out)
    return pl.pallas_call(
        store,
        name="store_gradients",
        out_shape=shapes,
        in_specs=[pl.BlockSpec(memory_space=pltpu.VMEM)] * 4,
        out_specs=[hbm] * 4,
        scratch_shapes=[sem((4,))],
    )(*grads)


def solution(mesh):
    pair = P("row", "col", None)
    bias = P(None, ("col", "row"), None)
    return jax.shard_map(
        on_device,
        mesh=mesh,
        in_specs=(pair, pair, pair, P("row", "col"), bias, pair),
        out_specs=(pair, pair, pair, bias),
        check_vma=False,
    )
```

```python
import jax
import jax.numpy as jnp
from jax import lax
from jax.experimental import pallas as pl
from jax.experimental.pallas import tpu as pltpu
from jax.sharding import PartitionSpec as P

MESH = pl.DeviceIdType.MESH
F32, BF16 = jnp.float32, jnp.bfloat16
SCALE = 32 ** -0.5
ROWS = 3
UNROLL = 6
NT = (((1,), (1,)), ((), ()))
TN = (((0,), (0,)), ((), ()))


def iota(shape, dim):
    return lax.broadcasted_iota(jnp.int32, shape, dim)


def dot(a, b):
    return jnp.dot(a, b, preferred_element_type=F32)


def zero_one(hit):
    return jnp.where(hit, 1.0, 0.0).astype(BF16)


def class_place(at):
    return ((at >> 1) & 3) * 16 + (at >> 4) * 4 + ((at >> 3) & 1) * 2 + (at & 1)


def swap_place(at):
    return ((at >> 5) & 3) * 128 + (at >> 7) * 32 + (at & 31)


def kernel(
    q_hbm, k_hbm, v_hbm, mask_hbm, bias_hbm, do_hbm,
    dq_hbm, dk_hbm, dv_hbm, dbias_hbm,
    dq_ref, dk_ref, dv_ref, dbias_ref, q_ref, k_ref, v_ref, mask_ref, bias_ref, do_ref,
    swap, kv_send, kv_recv, kv_roll, pen, qd_send, qd_recv, lhs, b_wide, b_send, b_all, b_f32, bias, d_bias,
    d_f32, d_send, d_recv, d_sum, e_recv, dkv_t, dkv_part, dkv_out, dkv_in, dkv_send, dkv_recv, dq_buf, dq_send, dq_recv,
    hello, in_sem, out_sem, b1_ss, b1_rs, kv_ss, kv_rs, qd_ss, qd_rs, b2_ss, b2_rs, sh_ss, sh_rs,
    d2_ss, d2_rs, x_sem, dq_ss, dq_rs, dkv_ss, dkv_rs, e_ss, e_rs,
):
    r, c = lax.axis_index("row"), lax.axis_index("col")
    z, xl = r // 2, r % 2
    xh, y, core = c // 8, (c // 2) % 4, c % 2
    x = xh * 2 + xl
    zq, kappa = z // 4, z % 4
    sibling = (r, c + 1 - 2 * core)

    def place(at_z, at_x, at_y):
        return (at_z * 2 + at_x % 2, (at_x // 2) * 8 + at_y * 2 + core)

    def yz(o):
        to_y, to_z = (y + o // 4) % 4, (z + (o % 4) * 4) % 16
        return to_y, to_z // 4, place(to_z, x, to_y)

    def yx(o):
        to_y, to_x = (y + o % 4) % 4, (x + o // 4) % 4
        return to_y, to_x, place(z, to_x, to_y)

    def yl(o):
        to_y, to_l = (y + o % 4) % 4, (xl + o // 4) % 2
        return to_y, to_l, place(z, xh * 2 + to_l, to_y)

    def along(dz):
        return place((z + dz + 16) % 16, x, y)

    def copy(src, dst, ss, rs, device):
        return pltpu.make_async_remote_copy(
            src_ref=src, dst_ref=dst, send_sem=ss, recv_sem=rs, device_id=device, device_id_type=MESH
        )

    def each(low, high, do):
        def body(o, carry):
            do(o)
            return carry

        lax.fori_loop(low, high, body, 0)

    loads = [
        pltpu.make_async_copy(src, dst, in_sem.at[j])
        for j, (src, dst) in enumerate((
            (bias_hbm, bias_ref), (k_hbm, k_ref), (v_hbm, v_ref), (mask_hbm, mask_ref), (q_hbm, q_ref), (do_hbm, do_ref),
        ))
    ]
    for load in loads:
        load.start()

    near = (1, -1, 2, -2)
    barrier = pltpu.get_barrier_semaphore()

    def greet(device):
        pl.semaphore_signal(barrier, inc=1, device_id=device, device_id_type=MESH)

    def greet_far(o):
        greet(place((z + (o // 4) * 4) % 16, x, (y + o % 4) % 4))

    each(4, 16, greet_far)
    for dz in near:
        greet(along(dz))
    each(1, 16, lambda o: greet(yx(o)[2]))

    @pl.when(core == 0)
    def _():
        greet(sibling)

    swap_mat = zero_one(swap_place(iota((512, 512), 0)) == iota((512, 512), 1))
    swap[...] = swap_mat
    loads[0].wait()
    wide = jnp.concatenate([bias_ref[h] for h in range(4)], axis=0)
    for at_x in range(2):
        turned = dot(wide[:, 512 * at_x:512 * (at_x + 1)], swap_mat)
        for part in range(4):
            b_wide[pl.ds((part % 2) * 4 + (part // 2) * 2 + at_x, 8, stride=8), :] = turned[:, 128 * part:128 * (part + 1)]
    b_send[...] = b_wide[...].astype(BF16).reshape(4, 16, 128)

    for load in loads[1:]:
        load.wait()
    spread = swap_mat[:256] + swap_mat[256:]
    low_lanes = iota((32, 128), 1) < 64
    mask_lane = (iota((8, 128), 1) >> 5) == y
    mask = mask_ref[...].astype(F32)
    tiles = []
    for half in range(2):
        part = mask[:, 32 * half:32 * (half + 1)]
        part = jnp.concatenate([part] * 4, axis=1)
        part = jnp.concatenate([part, jnp.zeros((8 - ROWS, 128), F32)], axis=0)
        tiles.append(jnp.where(mask_lane, part, 0.0))
    mask_tile = jnp.concatenate(tiles, axis=0).astype(BF16)
    for h in range(4):
        kv_send[h, 96:112, :] = mask_tile
    for i in range(ROWS):
        pairs = dot(jnp.concatenate([k_ref[i], v_ref[i]], axis=1), spread)
        for h in range(4):
            one = pairs[:, 128 * h:128 * (h + 1)]
            kv_send[h, 32 * i:32 * (i + 1), :] = jnp.where(low_lanes, one[:32], one[32:]).astype(BF16)
    order = zero_one(class_place(iota((64, 64), 0)) == iota((64, 64), 1))
    low8 = iota((8, 128), 1) < 64
    for i in range(ROWS):
        turned = dot(order, jnp.concatenate([q_ref[i], do_ref[i]], axis=1)).astype(BF16)
        pairs = dot(turned, spread)
        for h in range(4):
            one = pairs[:, 128 * h:128 * (h + 1)]
            for to_l in range(2):
                eight = [one[16 * a + 8 * to_l:16 * a + 8 * to_l + 8] for a in range(4)]
                parts = [jnp.where(low8, eight[2 * p], eight[2 * p + 1]) for p in range(2)]
                qd_send[to_l, h, 16 * i:16 * (i + 1), :] = jnp.concatenate(parts, axis=0).astype(BF16)

    pl.semaphore_wait(barrier, 12 + 15 + len(near) + core)

    @pl.when(core == 1)
    def _():
        pl.semaphore_signal(hello, inc=1, device_id=sibling, device_id_type=MESH)

    def b1(o):
        to_y, _, device = yz(o)
        return copy(b_send.at[to_y], b_all.at[kappa, y * 4 + zq], b1_ss.at[o], b1_rs.at[o], device)

    def kv(o):
        to_y, _, device = yx(o)
        return copy(kv_send.at[to_y], kv_recv.at[core, xl, xh * 4 + y], kv_ss.at[o], kv_rs.at[o], device)

    def qd(o):
        to_y, to_l, device = yl(o)
        return copy(qd_send.at[to_l, to_y], qd_recv.at[xl, y], qd_ss.at[o], qd_rs.at[o], device)

    each(1, 16, lambda o: b1(o).start())
    each(1, 16, lambda o: kv(o).start())
    each(1, 8, lambda o: qd(o).start())
    b_all[kappa, y * 4 + zq] = b_send[y]
    kv_recv[core, xl, xh * 4 + y] = kv_send[y]
    qd_recv[xl, y] = qd_send[xl, y]

    each(1, 16, lambda o: b1(o).wait_recv())

    def half_of(dz):
        return pl.ds(0, 8) if dz == 2 else pl.ds(8, 8)

    def b2(j):
        dz = near[j]
        mine = b_all.at[kappa]
        if dz in (2, -2):
            mine = mine.at[half_of(dz)]
        return copy(mine, mine, b2_ss.at[j], b2_rs.at[j], along(dz))

    for j in range(len(near)):
        b2(j).start()

    def share(part):
        slab = kv_recv.at[core, (xl + part) % 2]
        return copy(slab, slab, sh_ss.at[part], sh_rs.at[part], sibling)

    each(1, 4, lambda o: kv(o).wait_recv())
    each(8, 12, lambda o: kv(o).wait_recv())

    @pl.when(core == 0)
    def _():
        pl.semaphore_wait(hello, 1)

    share(0).start()
    each(4, 8, lambda o: kv(o).wait_recv())
    each(12, 16, lambda o: kv(o).wait_recv())
    share(1).start()

    each(1, 8, lambda o: qd(o).wait_recv())
    lane_part = iota((32, 128), 1) >> 5
    for row in range(2 * ROWS):
        i = row % ROWS
        plain = [qd_recv[row // ROWS, p, 16 * i:16 * (i + 1), :].astype(F32) for p in range(4)]
        rolled = [jnp.concatenate([one[:, 64:], one[:, :64]], axis=1) for one in plain]
        for a in range(4):
            at = 8 * (a // 2)
            straight = jnp.concatenate([one[at:at + 8] for one in plain], axis=0)
            crossed = jnp.concatenate([one[at:at + 8] for one in rolled], axis=0)
            for part in range(4):
                block = straight if part // 2 == a % 2 else crossed
                at_row = 128 * part + 32 * a
                lhs[row, at_row:at_row + 32, :] = jnp.where(lane_part == part, block, 0.0).astype(BF16)

    for part in range(2):
        share(part).wait_recv()
    for at_l in range(2):
        for g in range(4):
            seen = jnp.zeros((16, 128), F32)
            for u in range(4):
                seen = seen + kv_recv[g // 2, at_l, (g % 2) * 4 + u, 96:112, :].astype(F32)
            pen[at_l, :, 128 * g:128 * (g + 1)] = 1e9 * (seen - 1.0)
        for i in range(ROWS):
            block = kv_recv[:, at_l, :, 32 * i:32 * (i + 1), :]
            kv_roll[at_l * ROWS + i] = jnp.concatenate([block[..., 64:], block[..., :64]], axis=3).reshape(512, 128)

    for j in range(len(near)):
        b2(j).wait_recv()
    b_f32[...] = b_all[...].astype(F32).reshape(1024, 128)
    for m in range(8):
        bias[:, 128 * m:128 * (m + 1)] = b_f32[pl.ds(m, 128, stride=8), :]
    d_bias[...] = jnp.zeros_like(d_bias)

    def attention_row(at, carry):
        at_l, i = at // ROWS, at % ROWS
        left = lhs[at]
        right = kv_recv[:, at_l, :, pl.ds(pl.multiple_of(i * 32, 32), 32), :].reshape(512, 128)
        both = lax.dot_general(left, right, NT, preferred_element_type=F32)
        s_a = both[0:128] * SCALE + bias[:, :512] + pen[at_l, pl.ds(i, 1), :]
        s_b = both[256:384] * SCALE + bias[:, 512:] + pen[at_l, pl.ds(i + 8, 1), :]
        dp_a, dp_b = both[128:256], both[384:512]
        top = jnp.max(jnp.maximum(s_a, s_b), axis=1, keepdims=True)
        e_a, e_b = jnp.exp(s_a - top), jnp.exp(s_b - top)
        inv = 1.0 / jnp.sum(e_a + e_b, axis=1, keepdims=True)
        delta_row = jnp.sum(e_a * dp_a + e_b * dp_b, axis=1, keepdims=True) * inv
        p_a, p_b = e_a * inv, e_b * inv
        g_a, g_b = p_a * (dp_a - delta_row), p_b * (dp_b - delta_row)
        d_bias[:, :512] += g_a
        d_bias[:, 512:] += g_b
        g_a, g_b = g_a.astype(BF16), g_b.astype(BF16)
        stack = jnp.concatenate([g_a, p_a.astype(BF16), g_b, p_b.astype(BF16)], axis=0)
        dkv_t[at] = lax.dot_general(left, stack, TN, preferred_element_type=F32)
        dq_buf[at] = (dot(g_a, right) + dot(g_b, kv_roll[at])) * SCALE
        return carry

    lax.fori_loop(0, 2 * ROWS, attention_row, 0, unroll=UNROLL)
    for m in range(8):
        d_f32[pl.ds(m, 128, stride=8), :] = d_bias[:, 128 * m:128 * (m + 1)]
    d_send[...] = d_f32[...].astype(BF16).reshape(4, 16, 16, 128)

    def d2(j):
        dz = near[j]
        src, dst = d_send.at[(kappa + dz + 4) % 4], d_recv.at[{1: 0, -1: 1, 2: 2, -2: 2}[dz]]
        if dz in (2, -2):
            src, dst = src.at[half_of(dz)], dst.at[half_of(dz)]
        return copy(src, dst, d2_ss.at[j], d2_rs.at[j], along(dz))

    for j in range(len(near)):
        d2(j).start()

    for row in range(2 * ROWS):
        for b in range(4):
            turned = dkv_t[row, :, 128 * b:128 * (b + 1)].T.reshape(4, 32, 128)
            i = row % ROWS
            dkv_part[b // 2, row // ROWS, (b % 2) * 4:(b % 2) * 4 + 4, 32 * i:32 * (i + 1), :] = turned
    dkv_out[...] = dkv_part[1 - core].astype(BF16)
    cross = copy(dkv_out, dkv_in, x_sem.at[0], x_sem.at[1], sibling)
    cross.start()

    gather = zero_one(
        ((iota((512, 128), 0) >> 7) * 32 + (iota((512, 128), 0) & 127)) == iota((512, 128), 1)
    )
    gather = jnp.where((iota((512, 128), 0) & 127) < 32, gather, jnp.zeros_like(gather))
    packed = []
    for row in range(2 * ROWS):
        line = jnp.concatenate([dq_buf[row, 32 * a:32 * (a + 1)].astype(BF16) for a in range(4)], axis=1)
        packed.append(dot(line, gather))
    for to_l in range(2):
        for p in range(4):
            pieces = [packed[to_l * ROWS + i][8 * p:8 * p + 8] for i in range(ROWS)]
            dq_send[to_l, p] = jnp.concatenate(pieces + [jnp.zeros((8, 128), F32)], axis=0).astype(BF16)

    def dq(o):
        to_y, to_l, device = yl(o)
        return copy(dq_send.at[to_l, to_y], dq_recv.at[xl, y], dq_ss.at[o], dq_rs.at[o], device)

    each(1, 8, lambda o: dq(o).start())
    dq_recv[xl, y] = dq_send[xl, y]

    cross.wait_recv()
    dkv_send[...] = (dkv_part[core] + dkv_in[...].astype(F32)).astype(BF16)

    def dkv(o):
        to_y, to_x, device = yx(o)
        src = dkv_send.at[to_x % 2, (to_x // 2) * 4 + to_y]
        return copy(src, dkv_recv.at[x, y], dkv_ss.at[o], dkv_rs.at[o], device)

    each(1, 16, lambda o: dkv(o).start())
    dkv_recv[x, y] = dkv_send[xl, xh * 4 + y]

    for j in range(len(near)):
        d2(j).wait_recv()
    total = d_f32[pl.ds(pl.multiple_of(kappa * 256, 256), 256), :]
    for slot in range(3):
        total = total + d_recv[slot].astype(F32).reshape(256, 128)
    d_sum[...] = total.reshape(16, 16, 128).astype(BF16)

    def e(o):
        to_y, to_zq, device = yz(o)
        return copy(d_sum.at[to_y * 4 + to_zq], e_recv.at[y, zq], e_ss.at[o], e_rs.at[o], device)

    each(1, 16, lambda o: e(o).start())
    e_recv[y, zq] = d_sum[y * 4 + zq]

    each(1, 8, lambda o: dq(o).wait_recv())
    back = zero_one(iota((64, 64), 0) == class_place(iota((64, 64), 1)))
    heads = []
    for h in range(4):
        got = [dq_recv[at_l, h].astype(F32) for at_l in range(2)]
        heads.append(jnp.concatenate([got[at_l][8 * i:8 * i + 8] for i in range(ROWS) for at_l in range(2)], axis=0))
    heads = dot(jnp.concatenate(heads, axis=1).astype(BF16), swap[...]).astype(BF16)
    for i in range(ROWS):
        block = jnp.concatenate([heads[16 * i:16 * (i + 1), 128 * a:128 * (a + 1)] for a in range(4)], axis=0)
        dq_ref[i] = dot(back, block).astype(BF16)
    stores = [
        pltpu.make_async_copy(src, dst, out_sem.at[j])
        for j, (src, dst) in enumerate(((dq_ref, dq_hbm), (dk_ref, dk_hbm), (dv_ref, dv_hbm), (dbias_ref, dbias_hbm)))
    ]
    stores[0].start()

    each(1, 16, lambda o: dkv(o).wait_recv())
    k_lanes = ((iota((96, 128), 1) >> 5) & 1) == 0
    sums = []
    for h in range(4):
        one = sum(dkv_recv[at_x, h].astype(F32) for at_x in range(4))
        sums.append(jnp.where(k_lanes, one * SCALE, one).astype(BF16))
    heads = dot(jnp.concatenate(sums, axis=1), swap[...]).astype(BF16)
    for i in range(ROWS):
        for half in range(2):
            part = heads[32 * i:32 * (i + 1), 256 * half:256 * (half + 1)]
            dk_ref[i, 32 * half:32 * (half + 1), :] = part[:, :128]
            dv_ref[i, 32 * half:32 * (half + 1), :] = part[:, 128:]
    stores[1].start()
    stores[2].start()

    each(1, 16, lambda o: e(o).wait_recv())
    b_wide[...] = sum(e_recv[:, part].astype(F32) for part in range(4)).reshape(64, 128)
    for at_x in range(2):
        lines = [b_wide[pl.ds((part % 2) * 4 + (part // 2) * 2 + at_x, 8, stride=8), :] for part in range(4)]
        rest = jnp.concatenate(lines, axis=1)
        terms = []
        for _ in range(3):
            terms.append(rest.astype(BF16).astype(F32))
            rest = rest - terms[-1]
        turned = dot(jnp.concatenate(terms, axis=0).astype(BF16), swap[...])
        turned = turned[:8] + turned[8:16] + turned[16:]
        for h in range(4):
            dbias_ref[h, :, 512 * at_x:512 * (at_x + 1)] = turned[2 * h:2 * h + 2]
    stores[3].start()

    each(1, 16, lambda o: b1(o).wait_send())
    each(1, 16, lambda o: kv(o).wait_send())
    each(1, 8, lambda o: qd(o).wait_send())
    for j in range(len(near)):
        b2(j).wait_send()
        d2(j).wait_send()
    for part in range(2):
        share(part).wait_send()
    cross.wait_send()
    each(1, 16, lambda o: dkv(o).wait_send())
    each(1, 8, lambda o: dq(o).wait_send())
    each(1, 16, lambda o: e(o).wait_send())
    for one in stores:
        one.wait()


def store(*refs):
    ins, outs, sems = refs[:4], refs[4:8], refs[8]
    copies = [pltpu.make_async_copy(src, dst, sems.at[j]) for j, (src, dst) in enumerate(zip(ins, outs))]
    for one in copies:
        one.start()
    for one in copies:
        one.wait()


def on_device(queries, keys, values, pair_mask, tri_bias, grad_out):
    sem = pltpu.SemaphoreType.DMA
    hbm = pl.BlockSpec(memory_space=pltpu.HBM)
    tile = (16, 128)
    shapes = (
        jax.ShapeDtypeStruct(queries.shape, BF16),
        jax.ShapeDtypeStruct(keys.shape, BF16),
        jax.ShapeDtypeStruct(values.shape, BF16),
        jax.ShapeDtypeStruct(tri_bias.shape, F32),
    )
    grads = pl.pallas_call(
        kernel,
        name="attention_backward",
        out_shape=shapes,
        in_specs=[hbm] * 6,
        out_specs=[hbm] * 4,
        scratch_shapes=[
            pltpu.VMEM(queries.shape, BF16),
            pltpu.VMEM(keys.shape, BF16),
            pltpu.VMEM(values.shape, BF16),
            pltpu.VMEM(tri_bias.shape, F32),
            pltpu.VMEM(queries.shape, BF16),
            pltpu.VMEM(keys.shape, BF16),
            pltpu.VMEM(values.shape, BF16),
            pltpu.VMEM(pair_mask.shape, jnp.int32),
            pltpu.VMEM(tri_bias.shape, BF16),
            pltpu.VMEM(grad_out.shape, BF16),
            pltpu.VMEM((512, 512), BF16),
            pltpu.VMEM((4, 112, 128), BF16),
            pltpu.VMEM((2, 2, 8, 112, 128), BF16),
            pltpu.VMEM((2 * ROWS, 512, 128), BF16),
            pltpu.VMEM((2, 16, 512), F32),
            pltpu.VMEM((2, 4, 48, 128), BF16),
            pltpu.VMEM((2, 4, 48, 128), BF16),
            pltpu.VMEM((2 * ROWS, 512, 128), BF16),
            pltpu.VMEM((64, 128), F32),
            pltpu.VMEM((4,) + tile, BF16),
            pltpu.VMEM((4, 16) + tile, BF16),
            pltpu.VMEM((1024, 128), F32),
            pltpu.VMEM((128, 1024), F32),
            pltpu.VMEM((128, 1024), F32),
            pltpu.VMEM((1024, 128), F32),
            pltpu.VMEM((4, 16) + tile, BF16),
            pltpu.VMEM((3, 16) + tile, BF16),
            pltpu.VMEM((16,) + tile, BF16),
            pltpu.VMEM((4, 4) + tile, BF16),
            pltpu.VMEM((2 * ROWS, 128, 512), F32),
            pltpu.VMEM((2, 2, 8, 96, 128), F32),
            pltpu.VMEM((2, 8, 96, 128), BF16),
            pltpu.VMEM((2, 8, 96, 128), BF16),
            pltpu.VMEM((2, 8, 96, 128), BF16),
            pltpu.VMEM((4, 4, 96, 128), BF16),
            pltpu.VMEM((2 * ROWS, 128, 128), F32),
            pltpu.VMEM((2, 4, 32, 128), BF16),
            pltpu.VMEM((2, 4, 32, 128), BF16),
            pltpu.SemaphoreType.REGULAR, sem((6,)), sem((4,)),
            sem((16,)), sem((16,)), sem((16,)), sem((16,)), sem((8,)), sem((8,)), sem((4,)), sem((4,)), sem((2,)), sem((2,)),
            sem((4,)), sem((4,)), sem((2,)), sem((8,)), sem((8,)), sem((16,)), sem((16,)), sem((16,)), sem((16,)),
        ],
        compiler_params=pltpu.CompilerParams(
            collective_id=0, has_side_effects=True, vmem_limit_bytes=60 * 1024 * 1024
        ),
    )(queries, keys, values, pair_mask, tri_bias, grad_out)
    return pl.pallas_call(
        store,
        name="store_gradients",
        out_shape=shapes,
        in_specs=[pl.BlockSpec(memory_space=pltpu.VMEM)] * 4,
        out_specs=[hbm] * 4,
        scratch_shapes=[sem((4,))],
    )(*grads)


def solution(mesh):
    pair = P("row", "col", None)
    bias = P(None, ("col", "row"), None)
    return jax.shard_map(
        on_device,
        mesh=mesh,
        in_specs=(pair, pair, pair, P("row", "col"), bias, pair),
        out_specs=(pair, pair, pair, bias),
        check_vma=False,
    )
```

```python
import jax
import jax.numpy as jnp
from jax import lax
from jax.experimental import pallas as pl
from jax.experimental.pallas import tpu as pltpu
from jax.sharding import PartitionSpec as P

MESH = pl.DeviceIdType.MESH
F32, BF16 = jnp.float32, jnp.bfloat16
SCALE = 32 ** -0.5
ROWS = 3
UNROLL = 6
NT = (((1,), (1,)), ((), ()))
TN = (((0,), (0,)), ((), ()))


def iota(shape, dim):
    return lax.broadcasted_iota(jnp.int32, shape, dim)


def dot(a, b):
    return jnp.dot(a, b, preferred_element_type=F32)


def zero_one(hit):
    return jnp.where(hit, 1.0, 0.0).astype(BF16)


def query_place(at):
    return ((at >> 1) & 15) * 4 + (at >> 5) * 2 + (at & 1)


def grad_place(at):
    return (at >> 4) * 16 + ((at >> 1) & 3) * 4 + ((at >> 3) & 1) * 2 + (at & 1)


def swap_place(at):
    return ((at >> 5) & 3) * 128 + (at >> 7) * 32 + (at & 31)


def kernel(
    q_hbm, k_hbm, v_hbm, mask_hbm, bias_hbm, do_hbm,
    dq_hbm, dk_hbm, dv_hbm, dbias_hbm,
    dq_ref, dk_ref, dv_ref, dbias_ref, q_ref, k_ref, v_ref, mask_ref, bias_ref, do_ref,
    swap, kv_send, kv_recv, pen, qd_send, qd_recv, lhs, b_wide, b_send, b_all, b_f32, bias, d_bias,
    d_f32, d_send, d_recv, d_half, d_sum, e_recv, dkv_t, dkv_part, dkv_out, dkv_in, dkv_send, dkv_recv, dq_buf, dq_send, dq_recv,
    hello, in_sem, out_sem, b1_sem, kv_ss, kv_rs, qd_sem, b2_sem, sh_ss, sh_rs, d2_sem, x_sem, dq_sem, dkv_sem, e_sem,
):
    r, c = lax.axis_index("row"), lax.axis_index("col")
    z, xl = r // 2, r % 2
    xh, y, core = c // 8, (c // 2) % 4, c % 2
    x = xh * 2 + xl
    sibling = (r, c + 1 - 2 * core)

    def place(at_z, at_x, at_y):
        return (at_z * 2 + at_x % 2, (at_x // 2) * 8 + at_y * 2 + core)

    def yz(o):
        to_y, step = (y + o % 4) % 4, o // 4
        return to_y, step, place((z + 5 * step + step // 2) % 16, x, to_y)

    def yx(o):
        to_y, to_x = (y + o % 4) % 4, (x + o // 4) % 4
        return to_y, to_x, place(z, to_x, to_y)

    def yl(o):
        to_y, to_l = (y + o % 4) % 4, (xl + o // 4) % 2
        return to_y, to_l, place(z, xh * 2 + to_l, to_y)

    def along(dz):
        return place((z + dz + 16) % 16, x, y)

    def copy(src, dst, ss, rs, device):
        return pltpu.make_async_remote_copy(
            src_ref=src, dst_ref=dst, send_sem=ss, recv_sem=rs, device_id=device, device_id_type=MESH
        )

    def each(low, high, do):
        def body(o, carry):
            do(o)
            return carry

        lax.fori_loop(low, high, body, 0)

    def arrived(ref, sem):
        pltpu.make_async_remote_copy(
            src_ref=ref, dst_ref=ref, send_sem=sem, recv_sem=sem, device_id=sibling, device_id_type=MESH
        ).wait_recv()

    def left(ref, sem):
        pltpu.make_async_remote_copy(
            src_ref=ref, dst_ref=ref, send_sem=sem, recv_sem=sem, device_id=sibling, device_id_type=MESH
        ).wait_send()

    loads = [
        pltpu.make_async_copy(src, dst, in_sem.at[j])
        for j, (src, dst) in enumerate((
            (bias_hbm, bias_ref), (k_hbm, k_ref), (v_hbm, v_ref), (mask_hbm, mask_ref), (q_hbm, q_ref), (do_hbm, do_ref),
        ))
    ]
    for load in loads:
        load.start()

    near = (1, -1, 2, -2, 3, -3)
    hops = (0, 5, -5)
    barrier = pltpu.get_barrier_semaphore()

    def greet(device):
        pl.semaphore_signal(barrier, inc=1, device_id=device, device_id_type=MESH)

    each(4, 12, lambda o: greet(yz(o)[2]))
    for dz in near:
        greet(along(dz))
    each(1, 16, lambda o: greet(yx(o)[2]))

    @pl.when(core == 0)
    def _():
        greet(sibling)

    swap_mat = zero_one(swap_place(iota((512, 512), 0)) == iota((512, 512), 1))
    swap[...] = swap_mat
    loads[0].wait()
    wide = jnp.concatenate([bias_ref[h] for h in range(4)], axis=0)
    for at_x in range(2):
        turned = dot(wide[:, 512 * at_x:512 * (at_x + 1)], swap_mat)
        for part in range(4):
            b_wide[pl.ds((part % 2) * 4 + (part // 2) * 2 + at_x, 8, stride=8), :] = turned[:, 128 * part:128 * (part + 1)]
    b_send[...] = b_wide[...].astype(BF16).reshape(4, 16, 128)

    for load in loads[1:]:
        load.wait()
    spread = swap_mat[:256] + swap_mat[256:]
    low_lanes = iota((32, 128), 1) < 64
    mask_lane = (iota((8, 128), 1) >> 5) == y
    mask = mask_ref[...].astype(F32)
    tiles = []
    for half in range(2):
        part = mask[:, 32 * half:32 * (half + 1)]
        part = jnp.concatenate([part] * 4, axis=1)
        part = jnp.concatenate([part, jnp.zeros((8 - ROWS, 128), F32)], axis=0)
        tiles.append(jnp.where(mask_lane, part, 0.0))
    mask_tile = jnp.concatenate(tiles, axis=0).astype(BF16)
    for h in range(4):
        kv_send[h, 96:112, :] = mask_tile
    for i in range(ROWS):
        pairs = dot(jnp.concatenate([k_ref[i], v_ref[i]], axis=1), spread)
        for h in range(4):
            one = pairs[:, 128 * h:128 * (h + 1)]
            kv_send[h, 32 * i:32 * (i + 1), :] = jnp.where(low_lanes, one[:32], one[32:]).astype(BF16)
    order = zero_one(query_place(iota((64, 64), 0)) == iota((64, 64), 1))
    low16 = iota((16, 128), 1) < 64
    for i in range(ROWS):
        turned = dot(order, jnp.concatenate([q_ref[i], do_ref[i]], axis=1)).astype(BF16)
        pairs = dot(turned, spread)
        for h in range(4):
            one = pairs[:, 128 * h:128 * (h + 1)]
            for to_l in range(2):
                pair = jnp.where(low16, one[32 * to_l:32 * to_l + 16], one[32 * to_l + 16:32 * to_l + 32])
                qd_send[to_l, h, 16 * i:16 * (i + 1), :] = pair.astype(BF16)

    pl.semaphore_wait(barrier, 8 + 15 + len(near) + core)

    @pl.when(core == 1)
    def _():
        pl.semaphore_signal(hello, inc=1, device_id=sibling, device_id_type=MESH)

    def b1(o):
        to_y, _, device = yz(o)
        return copy(b_send.at[to_y], b_all.at[y, z], b1_sem.at[0], b1_sem.at[1], device)

    def kv(o):
        to_y, _, device = yx(o)
        return copy(kv_send.at[to_y], kv_recv.at[core, xl, xh * 4 + y], kv_ss.at[(o // 4) % 2], kv_rs.at[(o // 4) % 2], device)

    def qd(o):
        to_y, to_l, device = yl(o)
        return copy(qd_send.at[to_l, to_y], qd_recv.at[xl * 4 + y], qd_sem.at[0], qd_sem.at[1], device)

    each(1, 12, lambda o: b1(o).start())
    each(1, 16, lambda o: kv(o).start())
    each(1, 8, lambda o: qd(o).start())
    b_all[y, z] = b_send[y]
    kv_recv[core, xl, xh * 4 + y] = kv_send[y]
    qd_recv[xl * 4 + y] = qd_send[xl, y]

    arrived(b_all.at[0, pl.ds(0, 11)], b1_sem.at[1])

    def block_of(ref, dz, at_z):
        part = {3: pl.ds(0, 2), -3: pl.ds(2, 2)}.get(dz, slice(None))
        return ref.at[part, (at_z + 32) % 16]

    def b2(dz, hop):
        mine = block_of(b_all, dz, z + hop)
        return copy(mine, mine, b2_sem.at[0], b2_sem.at[1], along(dz))

    for hop in hops:
        for dz in near[:4]:
            b2(dz, hop).start()
    b2(3, -5).start()
    b2(-3, 5).start()

    def share(part):
        slab = kv_recv.at[core, (xl + part) % 2]
        return copy(slab, slab, sh_ss.at[part], sh_rs.at[part], sibling)

    arrived(kv_recv.at[core, xl, pl.ds(0, 7)], kv_rs.at[0])

    @pl.when(core == 0)
    def _():
        pl.semaphore_wait(hello, 1)

    share(0).start()
    arrived(kv_recv.at[core, 1 - xl], kv_rs.at[1])
    share(1).start()

    arrived(qd_recv.at[pl.ds(0, 7)], qd_sem.at[1])
    lane_part = iota((16, 128), 1) >> 5
    for row in range(2 * ROWS):
        i = row % ROWS
        for p in range(4):
            plain = qd_recv[row // ROWS * 4 + p, 16 * i:16 * (i + 1), :].astype(F32)
            rolled = pltpu.roll(plain, 64, 1)
            for half in range(2):
                for part in range(4):
                    at_row = 128 * part + 32 * p + 16 * half
                    block = plain if part // 2 == half else rolled
                    lhs[row, at_row:at_row + 16, :] = jnp.where(lane_part == part, block, 0.0).astype(BF16)

    for part in range(2):
        share(part).wait_recv()
    for at_l in range(2):
        for g in range(4):
            seen = jnp.zeros((16, 128), F32)
            for u in range(4):
                seen = seen + kv_recv[g // 2, at_l, (g % 2) * 4 + u, 96:112, :].astype(F32)
            pen[at_l, :, 128 * g:128 * (g + 1)] = 1e9 * (seen - 1.0)

    arrived(b_all.at[:, pl.ds(0, 13)], b2_sem.at[1])
    b_f32[...] = b_all[...].astype(F32).reshape(1024, 128)
    for m in range(8):
        bias[:, 128 * m:128 * (m + 1)] = b_f32[pl.ds(m, 128, stride=8), :]
    d_bias[...] = jnp.zeros_like(d_bias)

    def attention_row(at, carry):
        at_l, i = at // ROWS, at % ROWS
        left = lhs[at]
        right = kv_recv[:, at_l, :, pl.ds(pl.multiple_of(i * 32, 32), 32), :].reshape(512, 128)
        both = lax.dot_general(left, right, NT, preferred_element_type=F32)
        s_a = both[0:128] * SCALE + bias[:, :512] + pen[at_l, pl.ds(i, 1), :]
        s_b = both[256:384] * SCALE + bias[:, 512:] + pen[at_l, pl.ds(i + 8, 1), :]
        dp_a, dp_b = both[128:256], both[384:512]
        top = jnp.max(jnp.maximum(s_a, s_b), axis=1, keepdims=True)
        e_a, e_b = jnp.exp(s_a - top), jnp.exp(s_b - top)
        inv = 1.0 / jnp.sum(e_a + e_b, axis=1, keepdims=True)
        delta_row = jnp.sum(e_a * dp_a + e_b * dp_b, axis=1, keepdims=True) * inv
        p_a, p_b = e_a * inv, e_b * inv
        g_a, g_b = p_a * (dp_a - delta_row), p_b * (dp_b - delta_row)
        d_bias[:, :512] += g_a
        d_bias[:, 512:] += g_b
        g_a, g_b = g_a.astype(BF16), g_b.astype(BF16)
        stack = jnp.concatenate([g_a, p_a.astype(BF16), g_b, p_b.astype(BF16)], axis=0)
        dkv_t[at] = lax.dot_general(left, stack, TN, preferred_element_type=F32)
        dq_buf[at] = (dot(g_a, right) + pltpu.roll(dot(g_b, right), 64, 1)) * SCALE
        return carry

    lax.fori_loop(0, 2 * ROWS, attention_row, 0, unroll=UNROLL)
    for m in range(8):
        d_f32[pl.ds(m, 128, stride=8), :] = d_bias[:, 128 * m:128 * (m + 1)]
    d_send[...] = d_f32[...].astype(BF16).reshape(4, 16, 16, 128)

    def d2(dz, hop):
        src = block_of(d_send, {3: -3, -3: 3}.get(dz, dz), z + dz + hop)
        dst = d_recv.at[near.index(dz), hops.index(hop)] if dz in near[:4] else d_half.at[hops.index(hop) - 1]
        return copy(src, dst, d2_sem.at[0], d2_sem.at[1], along(dz))

    for hop in hops[::-1]:
        for dz in near[:4]:
            d2(dz, hop).start()
    d2(3, 5).start()
    d2(-3, -5).start()

    for row in range(2 * ROWS):
        for b in range(4):
            turned = dkv_t[row, :, 128 * b:128 * (b + 1)].T.reshape(4, 32, 128)
            i = row % ROWS
            dkv_part[b // 2, row // ROWS, (b % 2) * 4:(b % 2) * 4 + 4, 32 * i:32 * (i + 1), :] = turned
    dkv_out[...] = dkv_part[1 - core].astype(BF16)
    cross = copy(dkv_out, dkv_in, x_sem.at[0], x_sem.at[1], sibling)
    cross.start()

    gather = zero_one(
        ((iota((512, 128), 0) >> 7) * 32 + (iota((512, 128), 0) & 127)) == iota((512, 128), 1)
    )
    gather = jnp.where((iota((512, 128), 0) & 127) < 32, gather, jnp.zeros_like(gather))
    packed = []
    for row in range(2 * ROWS):
        groups = [jnp.concatenate([dq_buf[row, at:at + 8] for at in range(8 * g, 128, 32)], axis=0) for g in range(4)]
        line = jnp.concatenate(groups, axis=1).astype(BF16)
        packed.append(dot(line, gather))
    for to_l in range(2):
        for p in range(4):
            pieces = [packed[to_l * ROWS + i][8 * p:8 * p + 8] for i in range(ROWS)]
            dq_send[to_l, p] = jnp.concatenate(pieces + [jnp.zeros((8, 128), F32)], axis=0).astype(BF16)

    def dq(o):
        to_y, to_l, device = yl(o)
        return copy(dq_send.at[to_l, to_y], dq_recv.at[xl * 4 + y], dq_sem.at[0], dq_sem.at[1], device)

    each(1, 8, lambda o: dq(o).start())
    dq_recv[xl * 4 + y] = dq_send[xl, y]

    cross.wait_recv()
    dkv_send[...] = (dkv_part[core] + dkv_in[...].astype(F32)).astype(BF16)

    def dkv(o):
        to_y, to_x, device = yx(o)
        src = dkv_send.at[to_x % 2, (to_x // 2) * 4 + to_y]
        return copy(src, dkv_recv.at[x * 4 + y], dkv_sem.at[0], dkv_sem.at[1], device)

    each(1, 16, lambda o: dkv(o).start())
    dkv_recv[x * 4 + y] = dkv_send[xl, xh * 4 + y]

    arrived(d_send.at[:, pl.ds(0, 13)], d2_sem.at[1])
    for step, hop in enumerate(hops):
        at_z = (z + hop + 16) % 16
        for p in range(4):
            total = d_f32[pl.ds(pl.multiple_of(256 * p + 16 * at_z, 16), 16), :]
            for slot in range(4):
                total = total + d_recv[slot, step, p].astype(F32)
            if step and p // 2 == 2 - step:
                total = total + d_half[step - 1, p % 2].astype(F32)
            d_sum[step, p] = total.astype(BF16)

    def e(o):
        to_y, step, device = yz(o)
        return copy(d_sum.at[step, to_y], e_recv.at[y * 3 + step], e_sem.at[0], e_sem.at[1], device)

    each(1, 12, lambda o: e(o).start())
    e_recv[y * 3] = d_sum[0, y]

    arrived(dq_recv.at[pl.ds(0, 7)], dq_sem.at[1])
    back = zero_one(iota((64, 64), 0) == grad_place(iota((64, 64), 1)))
    heads = []
    for h in range(4):
        got = [dq_recv[at_l * 4 + h].astype(F32) for at_l in range(2)]
        heads.append(jnp.concatenate([got[at_l][8 * i:8 * i + 8] for i in range(ROWS) for at_l in range(2)], axis=0))
    heads = dot(jnp.concatenate(heads, axis=1).astype(BF16), swap[...]).astype(BF16)
    for i in range(ROWS):
        block = jnp.concatenate([heads[16 * i:16 * (i + 1), 128 * a:128 * (a + 1)] for a in range(4)], axis=0)
        dq_ref[i] = dot(back, block).astype(BF16)
    stores = [
        pltpu.make_async_copy(src, dst, out_sem.at[j])
        for j, (src, dst) in enumerate(((dq_ref, dq_hbm), (dk_ref, dk_hbm), (dv_ref, dv_hbm), (dbias_ref, dbias_hbm)))
    ]
    stores[0].start()

    arrived(dkv_recv.at[pl.ds(0, 15)], dkv_sem.at[1])
    k_lanes = ((iota((96, 128), 1) >> 5) & 1) == 0
    sums = []
    for h in range(4):
        one = sum(dkv_recv[at_x * 4 + h].astype(F32) for at_x in range(4))
        sums.append(jnp.where(k_lanes, one * SCALE, one).astype(BF16))
    heads = dot(jnp.concatenate(sums, axis=1), swap[...]).astype(BF16)
    for i in range(ROWS):
        for half in range(2):
            part = heads[32 * i:32 * (i + 1), 256 * half:256 * (half + 1)]
            dk_ref[i, 32 * half:32 * (half + 1), :] = part[:, :128]
            dv_ref[i, 32 * half:32 * (half + 1), :] = part[:, 128:]
    stores[1].start()
    stores[2].start()

    left(b_all.at[0, pl.ds(0, 11)], b1_sem.at[0])
    left(kv_recv.at[core, xl, pl.ds(0, 7)], kv_ss.at[0])
    left(kv_recv.at[core, 1 - xl], kv_ss.at[1])
    left(qd_recv.at[pl.ds(0, 7)], qd_sem.at[0])
    left(b_all.at[:, pl.ds(0, 13)], b2_sem.at[0])
    left(d_send.at[:, pl.ds(0, 13)], d2_sem.at[0])
    for part in range(2):
        share(part).wait_send()
    cross.wait_send()
    left(dq_recv.at[pl.ds(0, 7)], dq_sem.at[0])
    left(dkv_recv.at[pl.ds(0, 15)], dkv_sem.at[0])
    left(e_recv.at[pl.ds(0, 11)], e_sem.at[0])
    arrived(e_recv.at[pl.ds(0, 11)], e_sem.at[1])
    for h in range(4):
        b_wide[16 * h:16 * (h + 1), :] = sum(e_recv[3 * h + step].astype(F32) for step in range(3))
    for at_x in range(2):
        lines = [b_wide[pl.ds((part % 2) * 4 + (part // 2) * 2 + at_x, 8, stride=8), :] for part in range(4)]
        rest = jnp.concatenate(lines, axis=1)
        terms = []
        for _ in range(3):
            terms.append(rest.astype(BF16).astype(F32))
            rest = rest - terms[-1]
        turned = dot(jnp.concatenate(terms, axis=0).astype(BF16), swap[...])
        turned = turned[:8] + turned[8:16] + turned[16:]
        for h in range(4):
            dbias_ref[h, :, 512 * at_x:512 * (at_x + 1)] = turned[2 * h:2 * h + 2]
    stores[3].start()

    for one in stores:
        one.wait()


def store(*refs):
    ins, outs, sems = refs[:4], refs[4:8], refs[8]
    copies = [pltpu.make_async_copy(src, dst, sems.at[j]) for j, (src, dst) in enumerate(zip(ins, outs))]
    for one in copies:
        one.start()
    for one in copies:
        one.wait()


def on_device(queries, keys, values, pair_mask, tri_bias, grad_out):
    sem = pltpu.SemaphoreType.DMA
    hbm = pl.BlockSpec(memory_space=pltpu.HBM)
    tile = (16, 128)
    shapes = (
        jax.ShapeDtypeStruct(queries.shape, BF16),
        jax.ShapeDtypeStruct(keys.shape, BF16),
        jax.ShapeDtypeStruct(values.shape, BF16),
        jax.ShapeDtypeStruct(tri_bias.shape, F32),
    )
    grads = pl.pallas_call(
        kernel,
        name="attention_backward",
        out_shape=shapes,
        in_specs=[hbm] * 6,
        out_specs=[hbm] * 4,
        scratch_shapes=[
            pltpu.VMEM(queries.shape, BF16),
            pltpu.VMEM(keys.shape, BF16),
            pltpu.VMEM(values.shape, BF16),
            pltpu.VMEM(tri_bias.shape, F32),
            pltpu.VMEM(queries.shape, BF16),
            pltpu.VMEM(keys.shape, BF16),
            pltpu.VMEM(values.shape, BF16),
            pltpu.VMEM(pair_mask.shape, jnp.int32),
            pltpu.VMEM(tri_bias.shape, BF16),
            pltpu.VMEM(grad_out.shape, BF16),
            pltpu.VMEM((512, 512), BF16),
            pltpu.VMEM((4, 112, 128), BF16),
            pltpu.VMEM((2, 2, 8, 112, 128), BF16),
            pltpu.VMEM((2, 16, 512), F32),
            pltpu.VMEM((2, 4, 48, 128), BF16),
            pltpu.VMEM((8, 48, 128), BF16),
            pltpu.VMEM((2 * ROWS, 512, 128), BF16),
            pltpu.VMEM((64, 128), F32),
            pltpu.VMEM((4,) + tile, BF16),
            pltpu.VMEM((4, 16) + tile, BF16),
            pltpu.VMEM((1024, 128), F32),
            pltpu.VMEM((128, 1024), F32),
            pltpu.VMEM((128, 1024), F32),
            pltpu.VMEM((1024, 128), F32),
            pltpu.VMEM((4, 16) + tile, BF16),
            pltpu.VMEM((4, 3, 4) + tile, BF16),
            pltpu.VMEM((2, 2) + tile, BF16),
            pltpu.VMEM((3, 4) + tile, BF16),
            pltpu.VMEM((12,) + tile, BF16),
            pltpu.VMEM((2 * ROWS, 128, 512), F32),
            pltpu.VMEM((2, 2, 8, 96, 128), F32),
            pltpu.VMEM((2, 8, 96, 128), BF16),
            pltpu.VMEM((2, 8, 96, 128), BF16),
            pltpu.VMEM((2, 8, 96, 128), BF16),
            pltpu.VMEM((16, 96, 128), BF16),
            pltpu.VMEM((2 * ROWS, 128, 128), F32),
            pltpu.VMEM((2, 4, 32, 128), BF16),
            pltpu.VMEM((8, 32, 128), BF16),
            pltpu.SemaphoreType.REGULAR, sem((6,)), sem((4,)),
            sem((2,)), sem((2,)), sem((2,)), sem((2,)), sem((2,)), sem((2,)), sem((2,)), sem((2,)), sem((2,)), sem((2,)), sem((2,)), sem((2,)),
        ],
        compiler_params=pltpu.CompilerParams(
            collective_id=0, has_side_effects=True, vmem_limit_bytes=60 * 1024 * 1024
        ),
    )(queries, keys, values, pair_mask, tri_bias, grad_out)
    return pl.pallas_call(
        store,
        name="store_gradients",
        out_shape=shapes,
        in_specs=[pl.BlockSpec(memory_space=pltpu.VMEM)] * 4,
        out_specs=[hbm] * 4,
        scratch_shapes=[sem((4,))],
    )(*grads)


def solution(mesh):
    pair = P("row", "col", None)
    bias = P(None, ("col", "row"), None)
    return jax.shard_map(
        on_device,
        mesh=mesh,
        in_specs=(pair, pair, pair, P("row", "col"), bias, pair),
        out_specs=(pair, pair, pair, bias),
        check_vma=False,
    )
```

```python
import jax
import jax.numpy as jnp
from jax import lax
from jax.experimental import pallas as pl
from jax.experimental.pallas import tpu as pltpu
from jax.sharding import PartitionSpec as P

MESH = pl.DeviceIdType.MESH
F32, BF16 = jnp.float32, jnp.bfloat16
SCALE = 32 ** -0.5
ROWS = 3
UNROLL = 6
NT = (((1,), (1,)), ((), ()))
TN = (((0,), (0,)), ((), ()))


def iota(shape, dim):
    return lax.broadcasted_iota(jnp.int32, shape, dim)


def dot(a, b):
    return jnp.dot(a, b, preferred_element_type=F32)


def zero_one(hit):
    return jnp.where(hit, 1.0, 0.0).astype(BF16)


def query_place(at):
    return ((at >> 1) & 15) * 4 + (at >> 5) * 2 + (at & 1)


def grad_place(at):
    return (at >> 4) * 16 + ((at >> 1) & 3) * 4 + ((at >> 3) & 1) * 2 + (at & 1)


def swap_place(at):
    return ((at >> 5) & 3) * 128 + (at >> 7) * 32 + (at & 31)


def kernel(
    q_hbm, k_hbm, v_hbm, mask_hbm, bias_hbm, do_hbm,
    dq_hbm, dk_hbm, dv_hbm, dbias_hbm,
    dq_ref, dk_ref, dv_ref, dbias_ref, q_ref, k_ref, v_ref, mask_ref, bias_ref, do_ref,
    swap, kv_send, kv_recv, pen, qd_send, qd_recv, lhs, b_wide, b_send, b_all, both, stack, b_f32, bias, d_bias,
    d_f32, d_send, d_recv, d_half, d_sum, e_recv, dkv_t, dkv_part, dkv_out, dkv_in, dkv_send, dkv_recv, dq_buf, dq_send, dq_recv,
    hello, in_sem, out_sem, b1_sem, kv_ss, kv_rs, qd_sem, b2_sem, sh_ss, sh_rs, d2_sem, half_sem, x_sem, dq_sem, dkv_sem, e_sem,
):
    r, c = lax.axis_index("row"), lax.axis_index("col")
    z, xl = r // 2, r % 2
    xh, y, core = c // 8, (c // 2) % 4, c % 2
    x = xh * 2 + xl
    sibling = (r, c + 1 - 2 * core)

    def place(at_z, at_x, at_y):
        return (at_z * 2 + at_x % 2, (at_x // 2) * 8 + at_y * 2 + core)

    def yz(o):
        to_y, step = (y + o % 4) % 4, o // 4
        return to_y, step, place((z + 5 * step + step // 2) % 16, x, to_y)

    def yx(o):
        to_y, to_x = (y + o % 4) % 4, (x + o // 4) % 4
        return to_y, to_x, place(z, to_x, to_y)

    def yl(o):
        to_y, to_l = (y + o % 4) % 4, (xl + o // 4) % 2
        return to_y, to_l, place(z, xh * 2 + to_l, to_y)

    def along(dz):
        return place((z + dz + 16) % 16, x, y)

    def copy(src, dst, ss, rs, device):
        return pltpu.make_async_remote_copy(
            src_ref=src, dst_ref=dst, send_sem=ss, recv_sem=rs, device_id=device, device_id_type=MESH
        )

    def each(low, high, do):
        def body(o, carry):
            do(o)
            return carry

        lax.fori_loop(low, high, body, 0, unroll=True)

    def arrived(ref, sem):
        pltpu.make_async_remote_copy(
            src_ref=ref, dst_ref=ref, send_sem=sem, recv_sem=sem, device_id=sibling, device_id_type=MESH
        ).wait_recv()

    def left(ref, sem):
        pltpu.make_async_remote_copy(
            src_ref=ref, dst_ref=ref, send_sem=sem, recv_sem=sem, device_id=sibling, device_id_type=MESH
        ).wait_send()

    loads = [
        pltpu.make_async_copy(src, dst, in_sem.at[j])
        for j, (src, dst) in enumerate((
            (bias_hbm, bias_ref), (k_hbm, k_ref), (v_hbm, v_ref), (mask_hbm, mask_ref), (q_hbm, q_ref), (do_hbm, do_ref),
        ))
    ]
    for load in loads:
        load.start()

    near = (1, -1, 2, -2, 3, -3)
    hops = (0, 5, -5)
    barrier = pltpu.get_barrier_semaphore()

    def greet(device):
        pl.semaphore_signal(barrier, inc=1, device_id=device, device_id_type=MESH)

    each(4, 12, lambda o: greet(yz(o)[2]))
    for dz in near:
        greet(along(dz))
    each(1, 16, lambda o: greet(yx(o)[2]))

    @pl.when(core == 0)
    def _():
        greet(sibling)

    swap_mat = zero_one(swap_place(iota((512, 512), 0)) == iota((512, 512), 1))
    swap[...] = swap_mat
    loads[0].wait()
    wide = jnp.concatenate([bias_ref[h] for h in range(4)], axis=0)
    for at_x in range(2):
        turned = dot(wide[:, 512 * at_x:512 * (at_x + 1)], swap_mat)
        for part in range(4):
            b_wide[pl.ds((part % 2) * 4 + (part // 2) * 2 + at_x, 8, stride=8), :] = turned[:, 128 * part:128 * (part + 1)]
    b_send[...] = b_wide[...].astype(BF16).reshape(4, 16, 128)

    for load in loads[1:]:
        load.wait()
    spread = swap_mat[:256] + swap_mat[256:]
    low_lanes = iota((32, 128), 1) < 64
    mask_lane = (iota((8, 128), 1) >> 5) == y
    mask = mask_ref[...].astype(F32)
    tiles = []
    for half in range(2):
        part = mask[:, 32 * half:32 * (half + 1)]
        part = jnp.concatenate([part] * 4, axis=1)
        part = jnp.concatenate([part, jnp.zeros((8 - ROWS, 128), F32)], axis=0)
        tiles.append(jnp.where(mask_lane, part, 0.0))
    mask_tile = jnp.concatenate(tiles, axis=0).astype(BF16)
    for h in range(4):
        kv_send[h, 96:112, :] = mask_tile
    for i in range(ROWS):
        pairs = dot(jnp.concatenate([k_ref[i], v_ref[i]], axis=1), spread)
        for h in range(4):
            one = pairs[:, 128 * h:128 * (h + 1)]
            kv_send[h, 32 * i:32 * (i + 1), :] = jnp.where(low_lanes, one[:32], one[32:]).astype(BF16)
    order = zero_one(query_place(iota((64, 64), 0)) == iota((64, 64), 1))
    low16 = iota((16, 128), 1) < 64
    for i in range(ROWS):
        turned = dot(order, jnp.concatenate([q_ref[i], do_ref[i]], axis=1)).astype(BF16)
        pairs = dot(turned, spread)
        for h in range(4):
            one = pairs[:, 128 * h:128 * (h + 1)]
            for to_l in range(2):
                pair = jnp.where(low16, one[32 * to_l:32 * to_l + 16], one[32 * to_l + 16:32 * to_l + 32])
                qd_send[to_l, h, 16 * i:16 * (i + 1), :] = pair.astype(BF16)

    pl.semaphore_wait(barrier, 8 + 15 + len(near) + core)

    @pl.when(core == 1)
    def _():
        pl.semaphore_signal(hello, inc=1, device_id=sibling, device_id_type=MESH)

    def b1(o):
        to_y, _, device = yz(o)
        return copy(b_send.at[to_y], b_all.at[y, z], b1_sem.at[0], b1_sem.at[1 + o // 4], device)

    def kv(o):
        to_y, _, device = yx(o)
        return copy(kv_send.at[to_y], kv_recv.at[core, xl, xh * 4 + y], kv_ss.at[(o // 4) % 2], kv_rs.at[(o // 4) % 2], device)

    def qd(o):
        to_y, to_l, device = yl(o)
        return copy(qd_send.at[to_l, to_y], qd_recv.at[xl * 4 + y], qd_sem.at[0], qd_sem.at[1], device)

    each(4, 12, lambda o: b1(o).start())
    each(1, 4, lambda o: b1(o).start())
    each(1, 16, lambda o: kv(o).start())
    each(1, 8, lambda o: qd(o).start())
    b_all[y, z] = b_send[y]
    kv_recv[core, xl, xh * 4 + y] = kv_send[y]
    qd_recv[xl * 4 + y] = qd_send[xl, y]


    def block_of(ref, dz, at_z):
        part = {3: pl.ds(0, 2), -3: pl.ds(2, 2)}.get(dz, slice(None))
        return ref.at[part, (at_z + 32) % 16]

    def b2(dz, hop):
        mine = block_of(b_all, dz, z + hop)
        return copy(mine, mine, b2_sem.at[0], b2_sem.at[1], along(dz))

    for step, hop in enumerate(hops):
        arrived(b_all.at[0, pl.ds(0, 4 if step else 3)], b1_sem.at[(1, 3, 2)[step]])
        if hop:
            b2(-3 if hop == 5 else 3, hop).start()
        for dz in (2, -2, 1, -1):
            b2(dz, hop).start()

    def share(part):
        slab = kv_recv.at[core, (xl + part) % 2]
        return copy(slab, slab, sh_ss.at[part], sh_rs.at[part], sibling)

    arrived(kv_recv.at[core, xl, pl.ds(0, 7)], kv_rs.at[0])

    @pl.when(core == 0)
    def _():
        pl.semaphore_wait(hello, 1)

    share(0).start()
    arrived(kv_recv.at[core, 1 - xl], kv_rs.at[1])
    share(1).start()

    arrived(qd_recv.at[pl.ds(0, 7)], qd_sem.at[1])
    lane_part = iota((16, 128), 1) >> 5
    for row in range(2 * ROWS):
        i = row % ROWS
        for p in range(4):
            plain = qd_recv[row // ROWS * 4 + p, 16 * i:16 * (i + 1), :].astype(F32)
            rolled = pltpu.roll(plain, 64, 1)
            for half in range(2):
                for part in range(4):
                    at_row = 128 * part + 32 * p + 16 * half
                    block = plain if part // 2 == half else rolled
                    lhs[row, at_row:at_row + 16, :] = jnp.where(lane_part == part, block, 0.0).astype(BF16)

    for part in range(2):
        share(part).wait_recv()
    for at_l in range(2):
        for g in range(4):
            seen = jnp.zeros((16, 128), F32)
            for u in range(4):
                seen = seen + kv_recv[g // 2, at_l, (g % 2) * 4 + u, 96:112, :].astype(F32)
            pen[at_l, :, 128 * g:128 * (g + 1)] = 1e9 * (seen - 1.0)

    def keys_of(at):
        return kv_recv[:, at // ROWS, :, pl.ds(pl.multiple_of(at % ROWS * 32, 32), 32), :].reshape(512, 128)

    def products(at, carry):
        both[at] = lax.dot_general(lhs[at], keys_of(at), NT, preferred_element_type=F32)
        return carry

    lax.fori_loop(0, 2 * ROWS, products, 0, unroll=UNROLL)

    arrived(b_all.at[:, pl.ds(0, 13)], b2_sem.at[1])
    b_f32[...] = b_all[...].astype(F32).reshape(1024, 128)
    for m in range(8):
        bias[:, 128 * m:128 * (m + 1)] = b_f32[pl.ds(m, 128, stride=8), :]
    d_bias[...] = jnp.zeros_like(d_bias)

    def attention_row(at, carry):
        at_l, i = at // ROWS, at % ROWS
        s_a = both[at, 0:128] * SCALE + bias[:, :512] + pen[at_l, pl.ds(i, 1), :]
        s_b = both[at, 256:384] * SCALE + bias[:, 512:] + pen[at_l, pl.ds(i + 8, 1), :]
        dp_a, dp_b = both[at, 128:256], both[at, 384:512]
        top = jnp.max(jnp.maximum(s_a, s_b), axis=1, keepdims=True)
        e_a, e_b = jnp.exp(s_a - top), jnp.exp(s_b - top)
        inv = 1.0 / jnp.sum(e_a + e_b, axis=1, keepdims=True)
        delta_row = jnp.sum(e_a * dp_a + e_b * dp_b, axis=1, keepdims=True) * inv
        p_a, p_b = e_a * inv, e_b * inv
        g_a, g_b = p_a * (dp_a - delta_row), p_b * (dp_b - delta_row)
        d_bias[:, :512] += g_a
        d_bias[:, 512:] += g_b
        for part, one in enumerate((g_a, p_a, g_b, p_b)):
            stack[at, 128 * part:128 * (part + 1), :] = one.astype(BF16)
        return carry

    lax.fori_loop(0, 2 * ROWS, attention_row, 0, unroll=UNROLL)
    for m in range(8):
        d_f32[pl.ds(m, 128, stride=8), :] = d_bias[:, 128 * m:128 * (m + 1)]
    d_send[...] = d_f32[...].astype(BF16).reshape(4, 16, 16, 128)

    def d2(dz, hop):
        src = block_of(d_send, {3: -3, -3: 3}.get(dz, dz), z + dz + hop)
        dst = d_recv.at[near.index(dz), hops.index(hop)] if dz in near[:4] else d_half.at[hops.index(hop) - 1]
        step = hops.index(hop)
        arrival = d2_sem.at[1 + step] if dz in near[:4] else half_sem.at[step - 1]
        return copy(src, dst, d2_sem.at[0], arrival, along(dz))

    for hop in hops[::-1]:
        if hop:
            d2(3 if hop == 5 else -3, hop).start()
        for dz in (2, -2, 1, -1):
            d2(dz, hop).start()

    def row_grads(at, carry):
        right = keys_of(at)
        dkv_t[at] = lax.dot_general(lhs[at], stack[at], TN, preferred_element_type=F32)
        from_b = pltpu.roll(dot(stack[at, 256:384, :], right), 64, 1)
        dq_buf[at] = (dot(stack[at, 0:128, :], right) + from_b) * SCALE
        return carry

    lax.fori_loop(0, 2 * ROWS, row_grads, 0, unroll=UNROLL)

    for row in range(2 * ROWS):
        for b in range(4):
            turned = dkv_t[row, :, 128 * b:128 * (b + 1)].T.reshape(4, 32, 128)
            i = row % ROWS
            dkv_part[b // 2, row // ROWS, (b % 2) * 4:(b % 2) * 4 + 4, 32 * i:32 * (i + 1), :] = turned
    dkv_out[...] = dkv_part[1 - core].astype(BF16)
    cross = copy(dkv_out, dkv_in, x_sem.at[0], x_sem.at[1], sibling)
    cross.start()

    gather = zero_one(
        ((iota((512, 128), 0) >> 7) * 32 + (iota((512, 128), 0) & 127)) == iota((512, 128), 1)
    )
    gather = jnp.where((iota((512, 128), 0) & 127) < 32, gather, jnp.zeros_like(gather))
    packed = []
    for row in range(2 * ROWS):
        groups = [jnp.concatenate([dq_buf[row, at:at + 8] for at in range(8 * g, 128, 32)], axis=0) for g in range(4)]
        line = jnp.concatenate(groups, axis=1).astype(BF16)
        packed.append(dot(line, gather))
    for to_l in range(2):
        for p in range(4):
            pieces = [packed[to_l * ROWS + i][8 * p:8 * p + 8] for i in range(ROWS)]
            dq_send[to_l, p] = jnp.concatenate(pieces + [jnp.zeros((8, 128), F32)], axis=0).astype(BF16)

    def dq(o):
        to_y, to_l, device = yl(o)
        return copy(dq_send.at[to_l, to_y], dq_recv.at[xl * 4 + y], dq_sem.at[0], dq_sem.at[1], device)

    each(1, 8, lambda o: dq(o).start())
    dq_recv[xl * 4 + y] = dq_send[xl, y]

    cross.wait_recv()
    dkv_send[...] = (dkv_part[core] + dkv_in[...].astype(F32)).astype(BF16)

    def dkv(o):
        to_y, to_x, device = yx(o)
        src = dkv_send.at[to_x % 2, (to_x // 2) * 4 + to_y]
        return copy(src, dkv_recv.at[x * 4 + y], dkv_sem.at[0], dkv_sem.at[1], device)

    each(1, 16, lambda o: dkv(o).start())
    dkv_recv[x * 4 + y] = dkv_send[xl, xh * 4 + y]

    def e(o):
        to_y, step, device = yz(o)
        return copy(d_sum.at[step, to_y], e_recv.at[y * 3 + step], e_sem.at[0], e_sem.at[1], device)

    for step in (2, 1, 0):
        at_z = (z + hops[step] + 16) % 16
        arrived(d_recv.at[:, step], d2_sem.at[1 + step])
        if step:
            arrived(d_half.at[step - 1], half_sem.at[step - 1])
        for p in range(4):
            total = d_f32[pl.ds(pl.multiple_of(256 * p + 16 * at_z, 16), 16), :]
            for slot in range(4):
                total = total + d_recv[slot, step, p].astype(F32)
            if step and p // 2 == 2 - step:
                total = total + d_half[step - 1, p % 2].astype(F32)
            d_sum[step, p] = total.astype(BF16)
        each(4 * step if step else 1, 4 * step + 4, lambda o: e(o).start())
    e_recv[y * 3] = d_sum[0, y]

    arrived(dq_recv.at[pl.ds(0, 7)], dq_sem.at[1])
    back = zero_one(iota((64, 64), 0) == grad_place(iota((64, 64), 1)))
    heads = []
    for h in range(4):
        got = [dq_recv[at_l * 4 + h].astype(F32) for at_l in range(2)]
        heads.append(jnp.concatenate([got[at_l][8 * i:8 * i + 8] for i in range(ROWS) for at_l in range(2)], axis=0))
    heads = dot(jnp.concatenate(heads, axis=1).astype(BF16), swap[...]).astype(BF16)
    for i in range(ROWS):
        block = jnp.concatenate([heads[16 * i:16 * (i + 1), 128 * a:128 * (a + 1)] for a in range(4)], axis=0)
        dq_ref[i] = dot(back, block).astype(BF16)
    stores = [
        pltpu.make_async_copy(src, dst, out_sem.at[j])
        for j, (src, dst) in enumerate(((dq_ref, dq_hbm), (dk_ref, dk_hbm), (dv_ref, dv_hbm), (dbias_ref, dbias_hbm)))
    ]
    stores[0].start()

    arrived(dkv_recv.at[pl.ds(0, 15)], dkv_sem.at[1])
    k_lanes = ((iota((96, 128), 1) >> 5) & 1) == 0
    sums = []
    for h in range(4):
        one = sum(dkv_recv[at_x * 4 + h].astype(F32) for at_x in range(4))
        sums.append(jnp.where(k_lanes, one * SCALE, one).astype(BF16))
    heads = dot(jnp.concatenate(sums, axis=1), swap[...]).astype(BF16)
    for i in range(ROWS):
        for half in range(2):
            part = heads[32 * i:32 * (i + 1), 256 * half:256 * (half + 1)]
            dk_ref[i, 32 * half:32 * (half + 1), :] = part[:, :128]
            dv_ref[i, 32 * half:32 * (half + 1), :] = part[:, 128:]
    stores[1].start()
    stores[2].start()

    left(b_all.at[0, pl.ds(0, 11)], b1_sem.at[0])
    left(kv_recv.at[core, xl, pl.ds(0, 7)], kv_ss.at[0])
    left(kv_recv.at[core, 1 - xl], kv_ss.at[1])
    left(qd_recv.at[pl.ds(0, 7)], qd_sem.at[0])
    left(b_all.at[:, pl.ds(0, 13)], b2_sem.at[0])
    left(d_send.at[:, pl.ds(0, 13)], d2_sem.at[0])
    for part in range(2):
        share(part).wait_send()
    cross.wait_send()
    left(dq_recv.at[pl.ds(0, 7)], dq_sem.at[0])
    left(dkv_recv.at[pl.ds(0, 15)], dkv_sem.at[0])
    left(e_recv.at[pl.ds(0, 11)], e_sem.at[0])
    arrived(e_recv.at[pl.ds(0, 11)], e_sem.at[1])
    for h in range(4):
        b_wide[16 * h:16 * (h + 1), :] = sum(e_recv[3 * h + step].astype(F32) for step in range(3))
    for at_x in range(2):
        lines = [b_wide[pl.ds((part % 2) * 4 + (part // 2) * 2 + at_x, 8, stride=8), :] for part in range(4)]
        rest = jnp.concatenate(lines, axis=1)
        terms = []
        for _ in range(3):
            terms.append(rest.astype(BF16).astype(F32))
            rest = rest - terms[-1]
        turned = dot(jnp.concatenate(terms, axis=0).astype(BF16), swap[...])
        turned = turned[:8] + turned[8:16] + turned[16:]
        for h in range(4):
            dbias_ref[h, :, 512 * at_x:512 * (at_x + 1)] = turned[2 * h:2 * h + 2]
    stores[3].start()

    for one in stores:
        one.wait()


def store(*refs):
    ins, outs, sems = refs[:4], refs[4:8], refs[8]
    copies = [pltpu.make_async_copy(src, dst, sems.at[j]) for j, (src, dst) in enumerate(zip(ins, outs))]
    for one in copies:
        one.start()
    for one in copies:
        one.wait()


def on_device(queries, keys, values, pair_mask, tri_bias, grad_out):
    sem = pltpu.SemaphoreType.DMA
    hbm = pl.BlockSpec(memory_space=pltpu.HBM)
    tile = (16, 128)
    shapes = (
        jax.ShapeDtypeStruct(queries.shape, BF16),
        jax.ShapeDtypeStruct(keys.shape, BF16),
        jax.ShapeDtypeStruct(values.shape, BF16),
        jax.ShapeDtypeStruct(tri_bias.shape, F32),
    )
    grads = pl.pallas_call(
        kernel,
        name="attention_backward",
        out_shape=shapes,
        in_specs=[hbm] * 6,
        out_specs=[hbm] * 4,
        scratch_shapes=[
            pltpu.VMEM(queries.shape, BF16),
            pltpu.VMEM(keys.shape, BF16),
            pltpu.VMEM(values.shape, BF16),
            pltpu.VMEM(tri_bias.shape, F32),
            pltpu.VMEM(queries.shape, BF16),
            pltpu.VMEM(keys.shape, BF16),
            pltpu.VMEM(values.shape, BF16),
            pltpu.VMEM(pair_mask.shape, jnp.int32),
            pltpu.VMEM(tri_bias.shape, BF16),
            pltpu.VMEM(grad_out.shape, BF16),
            pltpu.VMEM((512, 512), BF16),
            pltpu.VMEM((4, 112, 128), BF16),
            pltpu.VMEM((2, 2, 8, 112, 128), BF16),
            pltpu.VMEM((2, 16, 512), F32),
            pltpu.VMEM((2, 4, 48, 128), BF16),
            pltpu.VMEM((8, 48, 128), BF16),
            pltpu.VMEM((2 * ROWS, 512, 128), BF16),
            pltpu.VMEM((64, 128), F32),
            pltpu.VMEM((4,) + tile, BF16),
            pltpu.VMEM((4, 16) + tile, BF16),
            pltpu.VMEM((2 * ROWS, 512, 512), F32),
            pltpu.VMEM((2 * ROWS, 512, 512), BF16),
            pltpu.VMEM((1024, 128), F32),
            pltpu.VMEM((128, 1024), F32),
            pltpu.VMEM((128, 1024), F32),
            pltpu.VMEM((1024, 128), F32),
            pltpu.VMEM((4, 16) + tile, BF16),
            pltpu.VMEM((4, 3, 4) + tile, BF16),
            pltpu.VMEM((2, 2) + tile, BF16),
            pltpu.VMEM((3, 4) + tile, BF16),
            pltpu.VMEM((12,) + tile, BF16),
            pltpu.VMEM((2 * ROWS, 128, 512), F32),
            pltpu.VMEM((2, 2, 8, 96, 128), F32),
            pltpu.VMEM((2, 8, 96, 128), BF16),
            pltpu.VMEM((2, 8, 96, 128), BF16),
            pltpu.VMEM((2, 8, 96, 128), BF16),
            pltpu.VMEM((16, 96, 128), BF16),
            pltpu.VMEM((2 * ROWS, 128, 128), F32),
            pltpu.VMEM((2, 4, 32, 128), BF16),
            pltpu.VMEM((8, 32, 128), BF16),
            pltpu.SemaphoreType.REGULAR, sem((6,)), sem((4,)),
            sem((4,)), sem((2,)), sem((2,)), sem((2,)), sem((2,)), sem((2,)), sem((2,)), sem((4,)), sem((2,)), sem((2,)), sem((2,)), sem((2,)), sem((2,)),
        ],
        compiler_params=pltpu.CompilerParams(
            collective_id=0, has_side_effects=True, vmem_limit_bytes=60 * 1024 * 1024
        ),
    )(queries, keys, values, pair_mask, tri_bias, grad_out)
    return pl.pallas_call(
        store,
        name="store_gradients",
        out_shape=shapes,
        in_specs=[pl.BlockSpec(memory_space=pltpu.VMEM)] * 4,
        out_specs=[hbm] * 4,
        scratch_shapes=[sem((4,))],
    )(*grads)


def solution(mesh):
    pair = P("row", "col", None)
    bias = P(None, ("col", "row"), None)
    return jax.shard_map(
        on_device,
        mesh=mesh,
        in_specs=(pair, pair, pair, P("row", "col"), bias, pair),
        out_specs=(pair, pair, pair, bias),
        check_vma=False,
    )
```

```python
import jax
import jax.numpy as jnp
from jax import lax
from jax.experimental import pallas as pl
from jax.experimental.pallas import tpu as pltpu
from jax.sharding import PartitionSpec as P

MESH = pl.DeviceIdType.MESH
F32, BF16 = jnp.float32, jnp.bfloat16
SCALE = 32 ** -0.5
ROWS = 3
UNROLL = 6
NT = (((1,), (1,)), ((), ()))


def iota(shape, dim):
    return lax.broadcasted_iota(jnp.int32, shape, dim)


def dot(a, b):
    return jnp.dot(a, b, preferred_element_type=F32)


def zero_one(hit):
    return jnp.where(hit, 1.0, 0.0).astype(BF16)


def query_place(at):
    return ((at >> 1) & 15) * 4 + (at >> 5) * 2 + (at & 1)


def grad_place(at):
    return (at >> 4) * 16 + ((at >> 1) & 3) * 4 + ((at >> 3) & 1) * 2 + (at & 1)


def swap_place(at):
    return ((at >> 5) & 3) * 128 + (at >> 7) * 32 + (at & 31)


def kernel(
    q_hbm, k_hbm, v_hbm, mask_hbm, bias_hbm, do_hbm,
    dq_hbm, dk_hbm, dv_hbm, dbias_hbm,
    dq_ref, dk_ref, dv_ref, dbias_ref, q_ref, k_ref, v_ref, mask_ref, bias_ref, do_ref,
    swap, kv_send, kv_recv, pen, qd_send, qd_recv, lhs, b_wide, b_send, b_all, both, stack, b_f32, bias, d_bias,
    d_f32, d_send, d_recv, d_half, d_sum, e_recv, lhs_t, dkv_part, dkv_out, dkv_in, dkv_send, dkv_recv, dq_buf, dq_send, dq_recv,
    hello, in_sem, out_sem, b1_sem, kv_ss, kv_rs, qd_sem, b2_sem, sh_ss, sh_rs, d2_sem, half_sem, x_sem, dq_sem, dkv_sem, e_sem,
):
    r, c = lax.axis_index("row"), lax.axis_index("col")
    z, xl = r // 2, r % 2
    xh, y, core = c // 8, (c // 2) % 4, c % 2
    x = xh * 2 + xl
    sibling = (r, c + 1 - 2 * core)

    def place(at_z, at_x, at_y):
        return (at_z * 2 + at_x % 2, (at_x // 2) * 8 + at_y * 2 + core)

    def yz(o):
        to_y, step = (y + o % 4) % 4, o // 4
        return to_y, step, place((z + 5 * step + step // 2) % 16, x, to_y)

    def yx(o):
        to_y, to_x = (y + o % 4) % 4, (x + o // 4) % 4
        return to_y, to_x, place(z, to_x, to_y)

    def yl(o):
        to_y, to_l = (y + o % 4) % 4, (xl + o // 4) % 2
        return to_y, to_l, place(z, xh * 2 + to_l, to_y)

    def along(dz):
        return place((z + dz + 16) % 16, x, y)

    def copy(src, dst, ss, rs, device):
        return pltpu.make_async_remote_copy(
            src_ref=src, dst_ref=dst, send_sem=ss, recv_sem=rs, device_id=device, device_id_type=MESH
        )

    def each(low, high, do):
        def body(o, carry):
            do(o)
            return carry

        lax.fori_loop(low, high, body, 0, unroll=True)

    def arrived(ref, sem):
        pltpu.make_async_remote_copy(
            src_ref=ref, dst_ref=ref, send_sem=sem, recv_sem=sem, device_id=sibling, device_id_type=MESH
        ).wait_recv()

    def left(ref, sem):
        pltpu.make_async_remote_copy(
            src_ref=ref, dst_ref=ref, send_sem=sem, recv_sem=sem, device_id=sibling, device_id_type=MESH
        ).wait_send()

    loads = [
        pltpu.make_async_copy(src, dst, in_sem.at[j])
        for j, (src, dst) in enumerate((
            (bias_hbm, bias_ref), (k_hbm, k_ref), (v_hbm, v_ref), (mask_hbm, mask_ref), (q_hbm, q_ref), (do_hbm, do_ref),
        ))
    ]
    for load in loads:
        load.start()

    near = (1, -1, 2, -2, 3, -3)
    hops = (0, 5, -5)
    barrier = pltpu.get_barrier_semaphore()

    def greet(device):
        pl.semaphore_signal(barrier, inc=1, device_id=device, device_id_type=MESH)

    each(4, 12, lambda o: greet(yz(o)[2]))
    for dz in near:
        greet(along(dz))
    each(1, 16, lambda o: greet(yx(o)[2]))

    @pl.when(core == 0)
    def _():
        greet(sibling)

    swap_mat = zero_one(swap_place(iota((512, 512), 0)) == iota((512, 512), 1))
    swap[...] = swap_mat
    loads[0].wait()
    wide = jnp.concatenate([bias_ref[h] for h in range(4)], axis=0)
    for at_x in range(2):
        turned = dot(wide[:, 512 * at_x:512 * (at_x + 1)], swap_mat)
        for part in range(4):
            b_wide[pl.ds((part % 2) * 4 + (part // 2) * 2 + at_x, 8, stride=8), :] = turned[:, 128 * part:128 * (part + 1)]
    b_send[...] = b_wide[...].astype(BF16).reshape(4, 16, 128)

    for load in loads[1:]:
        load.wait()
    spread = swap_mat[:256] + swap_mat[256:]
    low_lanes = iota((32, 128), 1) < 64
    mask_lane = (iota((8, 128), 1) >> 5) == y
    mask = mask_ref[...].astype(F32)
    tiles = []
    for half in range(2):
        part = mask[:, 32 * half:32 * (half + 1)]
        part = jnp.concatenate([part] * 4, axis=1)
        part = jnp.concatenate([part, jnp.zeros((8 - ROWS, 128), F32)], axis=0)
        tiles.append(jnp.where(mask_lane, part, 0.0))
    mask_tile = jnp.concatenate(tiles, axis=0).astype(BF16)
    for h in range(4):
        kv_send[h, 96:112, :] = mask_tile
    for i in range(ROWS):
        pairs = dot(jnp.concatenate([k_ref[i], v_ref[i]], axis=1), spread)
        for h in range(4):
            one = pairs[:, 128 * h:128 * (h + 1)]
            kv_send[h, 32 * i:32 * (i + 1), :] = jnp.where(low_lanes, one[:32], one[32:]).astype(BF16)
    order = zero_one(query_place(iota((64, 64), 0)) == iota((64, 64), 1))
    low16 = iota((16, 128), 1) < 64
    for i in range(ROWS):
        turned = dot(order, jnp.concatenate([q_ref[i], do_ref[i]], axis=1)).astype(BF16)
        pairs = dot(turned, spread)
        for h in range(4):
            one = pairs[:, 128 * h:128 * (h + 1)]
            for to_l in range(2):
                pair = jnp.where(low16, one[32 * to_l:32 * to_l + 16], one[32 * to_l + 16:32 * to_l + 32])
                qd_send[to_l, h, 16 * i:16 * (i + 1), :] = pair.astype(BF16)

    pl.semaphore_wait(barrier, 8 + 15 + len(near) + core)

    @pl.when(core == 1)
    def _():
        pl.semaphore_signal(hello, inc=1, device_id=sibling, device_id_type=MESH)

    def b1(o):
        to_y, _, device = yz(o)
        return copy(b_send.at[to_y], b_all.at[y, z], b1_sem.at[0], b1_sem.at[1 + o // 4], device)

    def kv(o):
        to_y, _, device = yx(o)
        return copy(kv_send.at[to_y], kv_recv.at[core, xl, xh * 4 + y], kv_ss.at[(o // 4) % 2], kv_rs.at[(o // 4) % 2], device)

    def qd(o):
        to_y, to_l, device = yl(o)
        return copy(qd_send.at[to_l, to_y], qd_recv.at[xl * 4 + y], qd_sem.at[0], qd_sem.at[1], device)

    each(4, 12, lambda o: b1(o).start())
    each(1, 4, lambda o: b1(o).start())
    each(1, 16, lambda o: kv(o).start())
    each(1, 8, lambda o: qd(o).start())
    b_all[y, z] = b_send[y]
    kv_recv[core, xl, xh * 4 + y] = kv_send[y]
    qd_recv[xl * 4 + y] = qd_send[xl, y]


    def block_of(ref, dz, at_z):
        part = {3: pl.ds(0, 2), -3: pl.ds(2, 2)}.get(dz, slice(None))
        return ref.at[part, (at_z + 32) % 16]

    def b2(dz, hop):
        mine = block_of(b_all, dz, z + hop)
        return copy(mine, mine, b2_sem.at[0], b2_sem.at[1], along(dz))

    for step, hop in enumerate(hops):
        arrived(b_all.at[0, pl.ds(0, 4 if step else 3)], b1_sem.at[(1, 3, 2)[step]])
        if hop:
            b2(-3 if hop == 5 else 3, hop).start()
        for dz in (2, -2, 1, -1):
            b2(dz, hop).start()

    def share(part):
        slab = kv_recv.at[core, (xl + part) % 2]
        return copy(slab, slab, sh_ss.at[part], sh_rs.at[part], sibling)

    arrived(kv_recv.at[core, xl, pl.ds(0, 7)], kv_rs.at[0])

    @pl.when(core == 0)
    def _():
        pl.semaphore_wait(hello, 1)

    share(0).start()
    arrived(kv_recv.at[core, 1 - xl], kv_rs.at[1])
    share(1).start()

    arrived(qd_recv.at[pl.ds(0, 7)], qd_sem.at[1])
    lane_part = iota((16, 128), 1) >> 5
    for row in range(2 * ROWS):
        i = row % ROWS
        for p in range(4):
            plain = qd_recv[row // ROWS * 4 + p, 16 * i:16 * (i + 1), :].astype(F32)
            rolled = pltpu.roll(plain, 64, 1)
            for half in range(2):
                for part in range(4):
                    at_row = 128 * part + 32 * p + 16 * half
                    block = plain if part // 2 == half else rolled
                    lhs[row, at_row:at_row + 16, :] = jnp.where(lane_part == part, block, 0.0).astype(BF16)

    for part in range(2):
        share(part).wait_recv()
    for at_l in range(2):
        for g in range(4):
            seen = jnp.zeros((16, 128), F32)
            for u in range(4):
                seen = seen + kv_recv[g // 2, at_l, (g % 2) * 4 + u, 96:112, :].astype(F32)
            pen[at_l, :, 128 * g:128 * (g + 1)] = 1e9 * (seen - 1.0)

    def keys_of(at):
        return kv_recv[:, at // ROWS, :, pl.ds(pl.multiple_of(at % ROWS * 32, 32), 32), :].reshape(512, 128)

    def products(at, carry):
        both[at] = lax.dot_general(lhs[at], keys_of(at), NT, preferred_element_type=F32)
        lhs_t[at] = lhs[at].T
        return carry

    lax.fori_loop(0, 2 * ROWS, products, 0, unroll=UNROLL)

    arrived(b_all.at[:, pl.ds(0, 13)], b2_sem.at[1])
    b_f32[...] = b_all[...].astype(F32).reshape(1024, 128)
    for m in range(8):
        bias[:, 128 * m:128 * (m + 1)] = b_f32[pl.ds(m, 128, stride=8), :]
    d_bias[...] = jnp.zeros_like(d_bias)

    def attention_row(at, carry):
        at_l, i = at // ROWS, at % ROWS
        s_a = both[at, 0:128] * SCALE + bias[:, :512] + pen[at_l, pl.ds(i, 1), :]
        s_b = both[at, 256:384] * SCALE + bias[:, 512:] + pen[at_l, pl.ds(i + 8, 1), :]
        dp_a, dp_b = both[at, 128:256], both[at, 384:512]
        top = jnp.max(jnp.maximum(s_a, s_b), axis=1, keepdims=True)
        e_a, e_b = jnp.exp(s_a - top), jnp.exp(s_b - top)
        inv = 1.0 / jnp.sum(e_a + e_b, axis=1, keepdims=True)
        delta_row = jnp.sum(e_a * dp_a + e_b * dp_b, axis=1, keepdims=True) * inv
        p_a, p_b = e_a * inv, e_b * inv
        g_a, g_b = p_a * (dp_a - delta_row), p_b * (dp_b - delta_row)
        d_bias[:, :512] += g_a
        d_bias[:, 512:] += g_b
        for part, one in enumerate((g_a, p_a, g_b, p_b)):
            stack[at, 128 * part:128 * (part + 1), :] = one.astype(BF16)
        return carry

    lax.fori_loop(0, 2 * ROWS, attention_row, 0, unroll=UNROLL)
    for m in range(8):
        d_f32[pl.ds(m, 128, stride=8), :] = d_bias[:, 128 * m:128 * (m + 1)]
    d_send[...] = d_f32[...].astype(BF16).reshape(4, 16, 16, 128)

    def d2(dz, hop):
        src = block_of(d_send, {3: -3, -3: 3}.get(dz, dz), z + dz + hop)
        dst = d_recv.at[near.index(dz), hops.index(hop)] if dz in near[:4] else d_half.at[hops.index(hop) - 1]
        step = hops.index(hop)
        arrival = d2_sem.at[1 + step] if dz in near[:4] else half_sem.at[step - 1]
        return copy(src, dst, d2_sem.at[0], arrival, along(dz))

    for hop in hops[::-1]:
        if hop:
            d2(3 if hop == 5 else -3, hop).start()
        for dz in (2, -2, 1, -1):
            d2(dz, hop).start()

    def cross(part):
        return copy(dkv_out.at[part], dkv_in.at[part], x_sem.at[part], x_sem.at[2 + part], sibling)

    for part in range(2):
        at_l = (xl + part) % 2
        for i in range(ROWS):
            at = at_l * ROWS + i
            grads = dot(lhs_t[at], stack[at])
            for b in range(4):
                turned = grads[:, 128 * b:128 * (b + 1)].T.reshape(4, 32, 128)
                dkv_part[b // 2, at_l, (b % 2) * 4:(b % 2) * 4 + 4, 32 * i:32 * (i + 1), :] = turned
        dkv_out[part] = dkv_part[1 - core, at_l].astype(BF16)
        cross(part).start()

    def row_grads(at, carry):
        right = keys_of(at)
        from_b = pltpu.roll(dot(stack[at, 256:384, :], right), 64, 1)
        dq_buf[at] = (dot(stack[at, 0:128, :], right) + from_b) * SCALE
        return carry

    lax.fori_loop(0, 2 * ROWS, row_grads, 0, unroll=UNROLL)

    gather = zero_one(
        ((iota((512, 128), 0) >> 7) * 32 + (iota((512, 128), 0) & 127)) == iota((512, 128), 1)
    )
    gather = jnp.where((iota((512, 128), 0) & 127) < 32, gather, jnp.zeros_like(gather))
    packed = []
    for row in range(2 * ROWS):
        groups = [jnp.concatenate([dq_buf[row, at:at + 8] for at in range(8 * g, 128, 32)], axis=0) for g in range(4)]
        line = jnp.concatenate(groups, axis=1).astype(BF16)
        packed.append(dot(line, gather))
    for to_l in range(2):
        for p in range(4):
            pieces = [packed[to_l * ROWS + i][8 * p:8 * p + 8] for i in range(ROWS)]
            dq_send[to_l, p] = jnp.concatenate(pieces + [jnp.zeros((8, 128), F32)], axis=0).astype(BF16)

    def dq(o):
        to_y, to_l, device = yl(o)
        return copy(dq_send.at[to_l, to_y], dq_recv.at[xl * 4 + y], dq_sem.at[0], dq_sem.at[1], device)

    each(1, 8, lambda o: dq(o).start())
    dq_recv[xl * 4 + y] = dq_send[xl, y]

    def dkv(o):
        to_y, to_x, device = yx(o)
        src = dkv_send.at[to_x % 2, (to_x // 2) * 4 + to_y]
        return copy(src, dkv_recv.at[x * 4 + y], dkv_sem.at[0], dkv_sem.at[1], device)

    for part in range(2):
        cross(part).wait_recv()
        at_l = (xl + part) % 2
        dkv_send[at_l] = (dkv_part[core, at_l] + dkv_in[part].astype(F32)).astype(BF16)
        each(4 if part else 1, 8 if part else 4, lambda o: dkv(o).start())
        each(12 if part else 8, 16 if part else 12, lambda o: dkv(o).start())
    dkv_recv[x * 4 + y] = dkv_send[xl, xh * 4 + y]

    def e(o):
        to_y, step, device = yz(o)
        return copy(d_sum.at[step, to_y], e_recv.at[y * 3 + step], e_sem.at[0], e_sem.at[1], device)

    for step in (2, 1, 0):
        at_z = (z + hops[step] + 16) % 16
        arrived(d_recv.at[:, step], d2_sem.at[1 + step])
        if step:
            arrived(d_half.at[step - 1], half_sem.at[step - 1])
        for p in range(4):
            total = d_f32[pl.ds(pl.multiple_of(256 * p + 16 * at_z, 16), 16), :]
            for slot in range(4):
                total = total + d_recv[slot, step, p].astype(F32)
            if step and p // 2 == 2 - step:
                total = total + d_half[step - 1, p % 2].astype(F32)
            d_sum[step, p] = total.astype(BF16)
        each(4 * step if step else 1, 4 * step + 4, lambda o: e(o).start())
    e_recv[y * 3] = d_sum[0, y]

    arrived(dq_recv.at[pl.ds(0, 7)], dq_sem.at[1])
    back = zero_one(iota((64, 64), 0) == grad_place(iota((64, 64), 1)))
    heads = []
    for h in range(4):
        got = [dq_recv[at_l * 4 + h].astype(F32) for at_l in range(2)]
        heads.append(jnp.concatenate([got[at_l][8 * i:8 * i + 8] for i in range(ROWS) for at_l in range(2)], axis=0))
    heads = dot(jnp.concatenate(heads, axis=1).astype(BF16), swap[...]).astype(BF16)
    for i in range(ROWS):
        block = jnp.concatenate([heads[16 * i:16 * (i + 1), 128 * a:128 * (a + 1)] for a in range(4)], axis=0)
        dq_ref[i] = dot(back, block).astype(BF16)
    stores = [
        pltpu.make_async_copy(src, dst, out_sem.at[j])
        for j, (src, dst) in enumerate(((dq_ref, dq_hbm), (dk_ref, dk_hbm), (dv_ref, dv_hbm), (dbias_ref, dbias_hbm)))
    ]
    stores[0].start()

    arrived(dkv_recv.at[pl.ds(0, 15)], dkv_sem.at[1])
    k_lanes = ((iota((96, 128), 1) >> 5) & 1) == 0
    sums = []
    for h in range(4):
        one = sum(dkv_recv[at_x * 4 + h].astype(F32) for at_x in range(4))
        sums.append(jnp.where(k_lanes, one * SCALE, one).astype(BF16))
    heads = dot(jnp.concatenate(sums, axis=1), swap[...]).astype(BF16)
    for i in range(ROWS):
        for half in range(2):
            part = heads[32 * i:32 * (i + 1), 256 * half:256 * (half + 1)]
            dk_ref[i, 32 * half:32 * (half + 1), :] = part[:, :128]
            dv_ref[i, 32 * half:32 * (half + 1), :] = part[:, 128:]
    stores[1].start()
    stores[2].start()

    left(b_all.at[0, pl.ds(0, 11)], b1_sem.at[0])
    left(kv_recv.at[core, xl, pl.ds(0, 7)], kv_ss.at[0])
    left(kv_recv.at[core, 1 - xl], kv_ss.at[1])
    left(qd_recv.at[pl.ds(0, 7)], qd_sem.at[0])
    left(b_all.at[:, pl.ds(0, 13)], b2_sem.at[0])
    left(d_send.at[:, pl.ds(0, 13)], d2_sem.at[0])
    for part in range(2):
        share(part).wait_send()
    for part in range(2):
        cross(part).wait_send()
    left(dq_recv.at[pl.ds(0, 7)], dq_sem.at[0])
    left(dkv_recv.at[pl.ds(0, 15)], dkv_sem.at[0])
    left(e_recv.at[pl.ds(0, 11)], e_sem.at[0])
    arrived(e_recv.at[pl.ds(0, 11)], e_sem.at[1])
    for h in range(4):
        b_wide[16 * h:16 * (h + 1), :] = sum(e_recv[3 * h + step].astype(F32) for step in range(3))
    for at_x in range(2):
        lines = [b_wide[pl.ds((part % 2) * 4 + (part // 2) * 2 + at_x, 8, stride=8), :] for part in range(4)]
        rest = jnp.concatenate(lines, axis=1)
        terms = []
        for _ in range(3):
            terms.append(rest.astype(BF16).astype(F32))
            rest = rest - terms[-1]
        turned = dot(jnp.concatenate(terms, axis=0).astype(BF16), swap[...])
        turned = turned[:8] + turned[8:16] + turned[16:]
        for h in range(4):
            dbias_ref[h, :, 512 * at_x:512 * (at_x + 1)] = turned[2 * h:2 * h + 2]
    stores[3].start()

    for one in stores:
        one.wait()


def store(*refs):
    ins, outs, sems = refs[:4], refs[4:8], refs[8]
    copies = [pltpu.make_async_copy(src, dst, sems.at[j]) for j, (src, dst) in enumerate(zip(ins, outs))]
    for one in copies:
        one.start()
    for one in copies:
        one.wait()


def on_device(queries, keys, values, pair_mask, tri_bias, grad_out):
    sem = pltpu.SemaphoreType.DMA
    hbm = pl.BlockSpec(memory_space=pltpu.HBM)
    tile = (16, 128)
    shapes = (
        jax.ShapeDtypeStruct(queries.shape, BF16),
        jax.ShapeDtypeStruct(keys.shape, BF16),
        jax.ShapeDtypeStruct(values.shape, BF16),
        jax.ShapeDtypeStruct(tri_bias.shape, F32),
    )
    grads = pl.pallas_call(
        kernel,
        name="attention_backward",
        out_shape=shapes,
        in_specs=[hbm] * 6,
        out_specs=[hbm] * 4,
        scratch_shapes=[
            pltpu.VMEM(queries.shape, BF16),
            pltpu.VMEM(keys.shape, BF16),
            pltpu.VMEM(values.shape, BF16),
            pltpu.VMEM(tri_bias.shape, F32),
            pltpu.VMEM(queries.shape, BF16),
            pltpu.VMEM(keys.shape, BF16),
            pltpu.VMEM(values.shape, BF16),
            pltpu.VMEM(pair_mask.shape, jnp.int32),
            pltpu.VMEM(tri_bias.shape, BF16),
            pltpu.VMEM(grad_out.shape, BF16),
            pltpu.VMEM((512, 512), BF16),
            pltpu.VMEM((4, 112, 128), BF16),
            pltpu.VMEM((2, 2, 8, 112, 128), BF16),
            pltpu.VMEM((2, 16, 512), F32),
            pltpu.VMEM((2, 4, 48, 128), BF16),
            pltpu.VMEM((8, 48, 128), BF16),
            pltpu.VMEM((2 * ROWS, 512, 128), BF16),
            pltpu.VMEM((64, 128), F32),
            pltpu.VMEM((4,) + tile, BF16),
            pltpu.VMEM((4, 16) + tile, BF16),
            pltpu.VMEM((2 * ROWS, 512, 512), F32),
            pltpu.VMEM((2 * ROWS, 512, 512), BF16),
            pltpu.VMEM((1024, 128), F32),
            pltpu.VMEM((128, 1024), F32),
            pltpu.VMEM((128, 1024), F32),
            pltpu.VMEM((1024, 128), F32),
            pltpu.VMEM((4, 16) + tile, BF16),
            pltpu.VMEM((4, 3, 4) + tile, BF16),
            pltpu.VMEM((2, 2) + tile, BF16),
            pltpu.VMEM((3, 4) + tile, BF16),
            pltpu.VMEM((12,) + tile, BF16),
            pltpu.VMEM((2 * ROWS, 128, 512), BF16),
            pltpu.VMEM((2, 2, 8, 96, 128), F32),
            pltpu.VMEM((2, 8, 96, 128), BF16),
            pltpu.VMEM((2, 8, 96, 128), BF16),
            pltpu.VMEM((2, 8, 96, 128), BF16),
            pltpu.VMEM((16, 96, 128), BF16),
            pltpu.VMEM((2 * ROWS, 128, 128), F32),
            pltpu.VMEM((2, 4, 32, 128), BF16),
            pltpu.VMEM((8, 32, 128), BF16),
            pltpu.SemaphoreType.REGULAR, sem((6,)), sem((4,)),
            sem((4,)), sem((2,)), sem((2,)), sem((2,)), sem((2,)), sem((2,)), sem((2,)), sem((4,)), sem((2,)), sem((4,)), sem((2,)), sem((2,)), sem((2,)),
        ],
        compiler_params=pltpu.CompilerParams(
            collective_id=0, has_side_effects=True, vmem_limit_bytes=60 * 1024 * 1024
        ),
    )(queries, keys, values, pair_mask, tri_bias, grad_out)
    return pl.pallas_call(
        store,
        name="store_gradients",
        out_shape=shapes,
        in_specs=[pl.BlockSpec(memory_space=pltpu.VMEM)] * 4,
        out_specs=[hbm] * 4,
        scratch_shapes=[sem((4,))],
    )(*grads)


def solution(mesh):
    pair = P("row", "col", None)
    bias = P(None, ("col", "row"), None)
    return jax.shard_map(
        on_device,
        mesh=mesh,
        in_specs=(pair, pair, pair, P("row", "col"), bias, pair),
        out_specs=(pair, pair, pair, bias),
        check_vma=False,
    )
```
